32 devices in a mesh: dp: 4 (over z), seq: 2 (over y), shard: 4 (over x, core).
Axes of the slice: x: 2, y: 2, z: 4, core: 2. Of those that a mesh axis runs over, the one named last changes fastest.
Arguments:
- tokens: bfloat16 [16, 1024, 768], P(('dp', 'shard'), 'seq'), may hold values from -18 to 18
- cotangent: bfloat16 [16, 1024, 768], P(('dp', 'shard'), 'seq'), may hold values from -6 to 6
- previous_logits: float32 [16, 1024, 12], P(('dp', 'shard'), 'seq'), may hold values from -2 to 2
- routes: int32 [16, 1024, 2], P(('dp', 'shard'), 'seq'), may hold values from 0 to 11, all different within a row
- priority: int32 [16, 2, 512], P(('dp', 'shard'), 'seq'), may hold values from 0 to 511, each once within a row
- attention_master: float32 [4, 768, 768], P(None, ('dp', 'seq', 'shard')), may hold values from -2 to 2
- vector_master: float32 [16, 768], P(None, ('dp', 'seq', 'shard')), may hold values from -6 to 6
- expert_master: float32 [8, 3, 768, 2048], P('shard', None, ('dp', 'seq')), may hold values from -5 to 5
- mixing_master: float32 [12, 12], replicated, may hold values from -1.75 to 1.75
- attention_first: float32 [4, 768, 768], P(None, ('dp', 'seq', 'shard')), may hold values from -16 to 16
- vector_first: float32 [16, 768], P(None, ('dp', 'seq', 'shard')), may hold values from -16 to 16
- expert_first: float32 [8, 3, 768, 2048], P('shard', None, ('dp', 'seq')), may hold values from -16 to 16
- mixing_first: float32 [12, 12], replicated, may hold values from -16 to 16
- attention_second: float32 [4, 768, 768], P(None, ('dp', 'seq', 'shard')), may hold values from 0 to 1.6384
- vector_second: float32 [16, 768], P(None, ('dp', 'seq', 'shard')), may hold values from 0 to 1.6384
- expert_second: float32 [8, 3, 768, 2048], P('shard', None, ('dp', 'seq')), may hold values from 0 to 1.6384
- mixing_second: float32 [12, 12], replicated, may hold values from 16.384 to 65.536
Outputs:
- block_output: bfloat16 [16, 1024, 768], P(('dp', 'shard'), 'seq')
- input_gradient: float32 [16, 1024, 768], P(('dp', 'shard'), 'seq')
- new_attention: float32 [4, 768, 768], P(None, ('dp', 'seq', 'shard'))
- new_vector: float32 [16, 768], P(None, ('dp', 'seq', 'shard'))
- new_expert: float32 [8, 3, 768, 2048], P('shard', None, ('dp', 'seq'))
- new_mixing: float32 [12, 12], replicated
- moment_attention: float32 [4, 768, 768], P(None, ('dp', 'seq', 'shard'))
- moment_vector: float32 [16, 768], P(None, ('dp', 'seq', 'shard'))
- moment_expert: float32 [8, 3, 768, 2048], P('shard', None, ('dp', 'seq'))
- moment_mixing: float32 [12, 12], replicated
- square_attention: float32 [4, 768, 768], P(None, ('dp', 'seq', 'shard'))
- square_vector: float32 [16, 768], P(None, ('dp', 'seq', 'shard'))
- square_expert: float32 [8, 3, 768, 2048], P('shard', None, ('dp', 'seq'))
- square_mixing: float32 [12, 12], replicated
- tensor_norms: float32 [2, 33], replicated
The draws below stay inside these ranges and needn't reach their ends.
Inputs may be any that keep to these rules, and one draw needn't show every extreme that they name: `routes`: each row names 2 different experts; 0 .. 7 are feed-forward experts, 8 the zero expert, 9 the copy expert, 10 and 11 the constant experts; every expert is named by some row. Each priority[s, c, :] is a permutation of 0 .. 511.
All inputs are finite; a program needn't handle non-finite values.
Results may differ from the reference program's by a relative error of at most 0.024.
The reference program's roundings to bfloat16 on the way count: a program that leaves them out, or rounds other values in their place, can miss the bound.
Values may be sent and summed in bfloat16 or wider, within the bound.
No kernel may reach another device: no remote copies, remote signals or barrier semaphores. Data moves between devices by JAX's collectives and lax.ppermute only.
A program may use at most 512 MiB of HBM per device.

```python
import math
import jax
import jax.numpy as jnp
from jax import lax

D = 768
HEADS = 12
HDIM = 64
FF = 2048
NFFN = 8
TOP = 2
STEP = 4
LEN = 1024
NEXP = 12
TOK_DEV = 512
CAP = 96
NSEQ = 16
TOKENS = 16384
N_SEQ = 2


def rising(count, lowest):
    return lowest + jnp.arange(count).astype(jnp.float32) / count


def base_values(key, shape):
    return jnp.clip(jax.random.normal(key, shape, jnp.float32), -4.0, 4.0)


def ramp_width():
    return rising(D, 0.5)


def draw_tokens(key, part):
    base_key, row_key, col_key = jax.random.split(key, 3)
    shape = (NSEQ, LEN, D)
    values = base_values(base_key, shape)
    row_scale = jnp.exp(jax.random.uniform(row_key, (NSEQ, LEN, 1), jnp.float32, -1.05, 1.25))
    col_scale = jnp.exp(jax.random.uniform(col_key, (1, 1, D), jnp.float32, -1.05, 1.25))
    return (0.35 * values * row_scale * col_scale).astype(jnp.bfloat16)


def draw_attention_master(key, part):
    values = base_values(key, (4, D, D))
    scales = jnp.array([1.2, 1.2, 1.0, 3.0], jnp.float32)[:, None, None] / jnp.sqrt(jnp.float32(D))
    return values * scales * ramp_width()[None, :, None]


def draw_vector_master(key, part):
    gain_key, const_key, router_key = jax.random.split(key, 3)
    ramp = ramp_width()[None, :]
    gains = (1.0 + 0.1 * base_values(gain_key, (2, D))) * ramp
    consts = 0.8 * base_values(const_key, (2, D)) * ramp
    router = 0.5 * base_values(router_key, (NEXP, D)) / jnp.sqrt(jnp.float32(D)) * ramp
    return jnp.concatenate([gains, consts, router], axis=0)


def draw_expert_master(key, part):
    values = base_values(key, (NFFN, 3, D, FF))
    scales = jnp.array([1.0 / D ** 0.5, 1.0 / D ** 0.5, 6.0 / FF ** 0.5], jnp.float32)[None, :, None, None]
    return values * scales * ramp_width()[None, None, :, None]


def second_moment(key, shape, ramp_axis):
    lowest = jnp.log(jnp.float32(1e-05 * TOKENS))
    highest = jnp.log(jnp.float32(0.0001 * TOKENS))
    base = jnp.exp(jax.random.uniform(key, shape, jnp.float32, lowest, highest))
    fall = jnp.exp(-jnp.log(9.0) * rising(D, 0.0))
    view = [1] * len(shape)
    view[ramp_axis] = D
    return base * fall.reshape(view)


def draw_attention_second(key, part):
    return second_moment(key, (4, D, D), 1)


def draw_vector_second(key, part):
    return second_moment(key, (4 + NEXP, D), 1)


def draw_expert_second(key, part):
    return second_moment(key, (NFFN, 3, D, FF), 2)


def steps_of(rng, dims, shards, smallest, top_value):
    loudness, own = 1.0, jax.random.fold_in(rng, 6)
    for dim, parts in shards:
        draws = jnp.exp(jax.random.uniform(jax.random.fold_in(own, dim), (parts,), jnp.float32, smallest / len(shards), top_value / len(shards)))
        loudness = loudness * jnp.repeat(draws, dims[dim] // parts).reshape([-1 if axis == dim else 1 for axis in range(len(dims))])
    return loudness


def different_ones(key, rows, number_of, top, lift):
    order = jax.random.permutation(jax.random.fold_in(key, 1), number_of)
    boost = order
    for power in range(3):
        boost = boost * boost // number_of
    boost = boost * lift // number_of
    tickets = jax.random.randint(jax.random.fold_in(key, 2), (rows, number_of), 0, 4096) + boost
    fixed_rows = jax.random.permutation(jax.random.fold_in(key, 3), rows)[jnp.arange(number_of) % rows]
    tickets = jnp.where(jnp.arange(rows)[:, None] == fixed_rows[None, :], 1 << 14, tickets)
    score = tickets * number_of + jnp.arange(number_of)
    return lax.top_k(score.astype(jnp.int32), top)[1].astype(jnp.int32)


def centred(key, shape, spread, most, cuts=(), held_as=jnp.bfloat16):
    values = spread * jax.random.normal(key, shape, jnp.float32)
    if cuts:
        values = values * steps_of(key, shape, cuts, -0.22, 0.18)
    return jnp.clip(values, -most, most).astype(held_as)


def setup_inputs(seed: int = 0) -> dict:
    streams_of = jax.random.split(jax.random.key(seed), 18)
    return {
        "tokens": draw_tokens(jax.random.fold_in(streams_of[17], 71), 0),
        "cotangent": centred(streams_of[1], (NSEQ, LEN, D), 1.0, 6.0, ((0, 16), (1, 2))),
        "previous_logits": centred(streams_of[2], (NSEQ, LEN, NEXP), 0.5, 2.0, ((0, 16), (1, 2)), jnp.float32),
        "routes": different_ones(streams_of[3], NSEQ * LEN, NEXP, TOP, 1365).reshape((NSEQ, LEN, TOP)),
        "priority": jax.vmap(lambda own: jax.random.permutation(own, TOK_DEV))(jax.random.split(streams_of[4], NSEQ * N_SEQ)).reshape((NSEQ, N_SEQ, TOK_DEV)).astype(jnp.int32),
        "attention_master": draw_attention_master(jax.random.fold_in(streams_of[17], 71), 0),
        "vector_master": draw_vector_master(jax.random.fold_in(streams_of[17], 71), 0),
        "expert_master": draw_expert_master(jax.random.fold_in(streams_of[17], 71), 0),
        "mixing_master": centred(streams_of[8], (NEXP, NEXP), NEXP ** -0.5, 1.75, (), jnp.float32),
        "attention_first": centred(streams_of[9], (4, D, D), (0.02 * TOKENS ** 0.5), 16.0, ((1, 32),), jnp.float32),
        "vector_first": centred(streams_of[10], (4 + NEXP, D), (0.02 * TOKENS ** 0.5), 16.0, ((1, 32),), jnp.float32),
        "expert_first": centred(streams_of[11], (NFFN, 3, D, FF), (0.02 * TOKENS ** 0.5), 16.0, ((0, 4), (2, 8)), jnp.float32),
        "mixing_first": centred(streams_of[12], (NEXP, NEXP), (0.02 * TOKENS ** 0.5), 16.0, (), jnp.float32),
        "attention_second": draw_attention_second(jax.random.fold_in(streams_of[17], 71), 0),
        "vector_second": draw_vector_second(jax.random.fold_in(streams_of[17], 71), 0),
        "expert_second": draw_expert_second(jax.random.fold_in(streams_of[17], 71), 0),
        "mixing_second": jnp.clip(jnp.exp(jax.random.uniform(streams_of[16], (NEXP, NEXP), jnp.float32, math.log(16.384), math.log(65.536))), 16.384, 65.536),
    }


beta_one = 0.9
beta_two = 0.999
adam_eps = 1e-06
weight_decay = 0.01
learn_rate = 0.25
norm_eps = 1e-06
rope_base = 10000.0

@jax.custom_vjp
def low(v):
    return lax.optimization_barrier(v.astype(jnp.bfloat16)).astype(jnp.float32)

@jax.custom_vjp
def low_back(v):
    return v

def low_keep(v):
    return (low(v), None)

def low_pass(kept, grad):
    return (grad,)

def back_keep(v):
    return (v, None)

def back_low(kept, grad):
    return (low(grad),)
low.defvjp(low_keep, low_pass)
low_back.defvjp(back_keep, back_low)

def exact_dot(left, right):
    return jnp.dot(left, right, precision=lax.Precision.HIGHEST, preferred_element_type=jnp.float32)

def exact_einsum(form, left, right):
    return jnp.einsum(form, left, right, precision=lax.Precision.HIGHEST, preferred_element_type=jnp.float32)

def root_norm(values, gain):
    return values * lax.rsqrt(lax.optimization_barrier(jnp.mean(values * values, axis=-1, keepdims=True)) + norm_eps) * gain

def rotary_tables(positions):
    freqs = rope_base ** (-jnp.arange(0, HDIM, 2).astype(jnp.float32) / HDIM)
    angles = positions[:, None] * freqs[None, :]
    cosine = jnp.concatenate([jnp.cos(angles), jnp.cos(angles)], axis=-1)
    sine_table = jnp.concatenate([jnp.sin(angles), jnp.sin(angles)], axis=-1)
    return (cosine, sine_table)

def rotate(values, cosine, sine_table):
    half_size = values.shape[-1] // 2
    turned = jnp.concatenate([-values[..., half_size:], values[..., :half_size]], axis=-1)
    return values * cosine[:, None, :] + turned * sine_table[:, None, :]

def softmax_rows(logits):
    row_top = lax.optimization_barrier(jnp.max(logits, axis=-1, keepdims=True))
    expd_values = jnp.exp(logits - row_top)
    return expd_values / lax.optimization_barrier(jnp.sum(expd_values, axis=-1, keepdims=True))

def swiglu(gate_pre, up_pre):
    return gate_pre * jax.nn.sigmoid(gate_pre) * up_pre

def placement(route_rows, order_rows, capacity):
    hits = lax.optimization_barrier(jnp.sum(jax.nn.one_hot(route_rows, NEXP, dtype=jnp.float32), axis=-2))
    before = (order_rows[:, None, :] < order_rows[:, :, None]).astype(jnp.float32)
    counts = exact_einsum('gtu,gue->gte', before, hits)
    slot_counts = jnp.take_along_axis(counts, route_rows, axis=-1)
    kept_mask = (route_rows < NFFN) & (slot_counts < capacity)
    return (slot_counts, kept_mask)

def forward(params, inputs, previous, route_rows, kept_mask, positions):
    attention_w, vector_w, expert_w, mixing_w = params
    attention = low(attention_w)
    vectors = low(vector_w)
    experts = low(expert_w)
    cosine, sine_table = rotary_tables(positions)
    normed = low(root_norm(inputs, vectors[0]))
    query_pre = low_back(exact_dot(normed, attention[0])).reshape(LEN, HEADS, HDIM)
    key_pre = low_back(exact_dot(normed, attention[1])).reshape(LEN, HEADS, HDIM)
    query = low_back(low(rotate(query_pre, cosine, sine_table)))
    keys_all = low_back(low(rotate(key_pre, cosine, sine_table)))
    values_all = low_back(low(exact_dot(normed, attention[2]))).reshape(LEN, HEADS, HDIM)
    scores = low_back(exact_einsum('qhd,khd->hqk', query, keys_all) * HDIM ** (-0.5))
    causal = positions[:, None] >= positions[None, :]
    scores = jnp.where(causal[None], scores, -1e+30)
    weights_soft = softmax_rows(scores)
    mixed = exact_einsum('hqk,khd->qhd', low(weights_soft), values_all).reshape(LEN, D)
    mixed = low_back(low(mixed))
    branch = low_back(exact_dot(mixed, attention[3]))
    resid = inputs + branch
    normed_two = root_norm(resid, vectors[1])
    expert_in = low(normed_two)
    logits = exact_dot(expert_in, vectors[4:].T) + exact_dot(previous, mixing_w)
    gates = softmax_rows(logits)
    picked = jnp.take_along_axis(gates, route_rows, axis=1)
    chosen = []
    for which_slot in range(TOP):
        route_col = route_rows[:, which_slot][:, None]
        entry = jnp.where(route_col == NFFN + 1, normed_two, 0.0)
        entry = entry + jnp.where(route_col == NFFN + 2, vectors[2][None, :], 0.0)
        entry = entry + jnp.where(route_col == NFFN + 3, vectors[3][None, :], 0.0)
        chosen.append(entry)
    for expert_index in range(NFFN):
        expert_view = low_back(expert_in)
        gate_pre = low_back(exact_dot(expert_view, experts[expert_index, 0]))
        up_pre = low_back(exact_dot(expert_view, experts[expert_index, 1]))
        hidden = low(swiglu(gate_pre, up_pre))
        result = lax.dot_general(hidden, experts[expert_index, 2], (((1,), (1,)), ((), ())), precision=lax.Precision.HIGHEST, preferred_element_type=jnp.float32)
        result = low_back(low(result))
        for which_slot in range(TOP):
            usage = (route_rows[:, which_slot] == expert_index) & kept_mask[:, which_slot]
            chosen[which_slot] = chosen[which_slot] + jnp.where(usage[:, None], result, 0.0)
    mixture = picked[:, 0:1] * chosen[0]
    for which_slot in range(1, TOP):
        mixture = mixture + picked[:, which_slot:which_slot + 1] * chosen[which_slot]
    return resid + mixture

def moments(weight, first, second, grad):
    first_new = beta_one * first + (1.0 - beta_one) * grad
    second_new = beta_two * second + (1.0 - beta_two) * grad * grad
    step_value = first_new / (1.0 - beta_one ** STEP) / (jnp.sqrt(second_new / (1.0 - beta_two ** STEP)) + adam_eps) + weight_decay * weight
    return (first_new, second_new, step_value)

def tensor_squares(attention_x, vector_x, expert_x):
    vector_parts = jnp.stack([jnp.sum(vector_x[0] * vector_x[0]), jnp.sum(vector_x[1] * vector_x[1]), jnp.sum(vector_x[2:4] * vector_x[2:4]), jnp.sum(vector_x[4:] * vector_x[4:])])
    return jnp.concatenate([lax.optimization_barrier(jnp.sum(attention_x * attention_x, axis=(1, 2))), vector_parts, lax.optimization_barrier(jnp.sum(expert_x * expert_x, axis=(2, 3))).reshape(-1)])

def apply_ratio(weights, steps, ratios):
    attention_w, vector_w, expert_w, mixing_w = weights
    attention_s, vector_s, expert_s, mixing_s = steps
    attention_ratio = ratios[0:4][:, None, None]
    vector_ratio = jnp.concatenate([ratios[4:6], jnp.broadcast_to(ratios[6:7], (2,)), jnp.broadcast_to(ratios[7:8], (vector_w.shape[0] - 4,))])[:, None]
    expert_ratio = ratios[8:8 + 3 * NFFN].reshape(NFFN, 3)[:, :, None, None]
    mixing_ratio = ratios[8 + 3 * NFFN]
    return (attention_w - learn_rate * attention_ratio * attention_s, vector_w - learn_rate * vector_ratio * vector_s, expert_w - learn_rate * expert_ratio * expert_s, mixing_w - learn_rate * mixing_ratio * mixing_s)

def reference(tokens, cotangent, previous_logits, routes, priority, attention_master, vector_master, expert_master, mixing_master, attention_first, vector_first, expert_first, mixing_first, attention_second, vector_second, expert_second, mixing_second):
    params = (attention_master, vector_master, expert_master, mixing_master)
    positions = jnp.arange(LEN).astype(jnp.float32)

    def one_sequence(totals, inputs):
        seq_tokens, seq_cot, seq_prev, seq_routes, seq_order = inputs
        grouped = seq_routes.reshape(N_SEQ, TOK_DEV, TOP)
        unused, kept_mask = placement(grouped, seq_order, CAP)
        kept_mask = kept_mask.reshape(LEN, TOP)

        def run(weights, values):
            return forward(weights, values, seq_prev, seq_routes, kept_mask, positions)
        output, pull = jax.vjp(run, params, seq_tokens.astype(jnp.float32))
        grads, input_grad = pull(seq_cot.astype(jnp.float32))
        totals = jax.tree.map(lambda first, second: first + second, totals, grads)
        return (totals, (output.astype(jnp.bfloat16), input_grad))
    zeros_tree = jax.tree.map(jnp.zeros_like, params)
    grads, (outputs, input_grads) = lax.scan(one_sequence, zeros_tree, (tokens, cotangent, previous_logits, routes, priority))
    attention_grad, vector_grad, expert_grad, mixing_grad = grads
    attention_m, attention_s, attention_u = moments(attention_master, attention_first, attention_second, attention_grad)
    vector_m, vector_s, vector_u = moments(vector_master, vector_first, vector_second, vector_grad)
    expert_m, expert_s, expert_u = moments(expert_master, expert_first, expert_second, expert_grad)
    mixing_m, mixing_s, mixing_u = moments(mixing_master, mixing_first, mixing_second, mixing_grad)
    weight_sq = jnp.concatenate([tensor_squares(attention_master, vector_master, expert_master), jnp.sum(mixing_master * mixing_master)[None]])
    step_sq = jnp.concatenate([tensor_squares(attention_u, vector_u, expert_u), jnp.sum(mixing_u * mixing_u)[None]])
    tensor_norms = jnp.sqrt(jnp.stack([weight_sq, step_sq]))
    ratios = tensor_norms[0] / (tensor_norms[1] + norm_eps)
    new_attention, new_vector, new_expert, new_mixing = apply_ratio(params, (attention_u, vector_u, expert_u, mixing_u), ratios)
    return (outputs, input_grads, new_attention, new_vector, new_expert, new_mixing, attention_m, vector_m, expert_m, mixing_m, attention_s, vector_s, expert_s, mixing_s, tensor_norms)
```

```python
import jax
import jax.numpy as jnp
from jax import lax
from jax.sharding import PartitionSpec as P

HEADS = 12
HDIM = 64
NFFN = 8
TOP = 2
STEP = 4
NEXP = 12

beta_one = 0.9
beta_two = 0.999
adam_eps = 1e-06
weight_decay = 0.01
learn_rate = 0.25
norm_eps = 1e-06
rope_base = 10000.0

bf16 = jnp.bfloat16
f32 = jnp.float32


def exact_dot(left, right):
    return jnp.dot(left, right, precision=lax.Precision.HIGHEST, preferred_element_type=f32)


def dot_nn(left, right):
    return lax.dot_general(left, right, (((1,), (0,)), ((), ())), preferred_element_type=f32)


def dot_nt(left, right):
    return lax.dot_general(left, right, (((1,), (1,)), ((), ())), preferred_element_type=f32)


def dot_tn(left, right):
    return lax.dot_general(left, right, (((0,), (0,)), ((), ())), preferred_element_type=f32)


def rotary_tables(positions):
    freqs = rope_base ** (-jnp.arange(0, HDIM, 2).astype(f32) / HDIM)
    angles = positions[:, None] * freqs[None, :]
    cosine = jnp.concatenate([jnp.cos(angles), jnp.cos(angles)], axis=-1)
    sine_table = jnp.concatenate([jnp.sin(angles), jnp.sin(angles)], axis=-1)
    return (cosine, sine_table)


def rotate(values, cosine, sine_table):
    half_size = values.shape[-1] // 2
    turned = jnp.concatenate([-values[..., half_size:], values[..., :half_size]], axis=-1)
    return values * cosine[:, None, :] + turned * sine_table[:, None, :]


def rotate_back(values, cosine, sine_table):
    half_size = values.shape[-1] // 2
    scaled = values * sine_table[:, None, :]
    turned = jnp.concatenate([scaled[..., half_size:], -scaled[..., :half_size]], axis=-1)
    return values * cosine[:, None, :] + turned


def softmax_rows(logits):
    row_top = jnp.max(logits, axis=-1, keepdims=True)
    expd_values = jnp.exp(logits - row_top)
    return expd_values / jnp.sum(expd_values, axis=-1, keepdims=True)


def moments(weight, first, second, grad):
    first_new = beta_one * first + (1.0 - beta_one) * grad
    second_new = beta_two * second + (1.0 - beta_two) * grad * grad
    step_value = (
        first_new
        / (1.0 - beta_one**STEP)
        / (jnp.sqrt(second_new / (1.0 - beta_two**STEP)) + adam_eps)
        + weight_decay * weight
    )
    return (first_new, second_new, step_value)


def swap_seq(value):
    return lax.ppermute(value, "seq", [(0, 1), (1, 0)])


def in_order(own, other, which, axis):
    low = jnp.where(which == 0, own, other)
    high = jnp.where(which == 0, other, own)
    return jnp.concatenate([low, high], axis=axis)


def pairs_dp(count, step):
    return [(i, (i + step) % count) for i in range(count)]


def pairs_x(count, step):
    return [(i, (i + 2 * step) % count) for i in range(count)]


def pairs_core(count):
    return [(i, i ^ 1) for i in range(count)]


def gather_steps(value, axis_name, pairs_of, place, count):
    out = jnp.zeros((count,) + value.shape, value.dtype)
    out = lax.dynamic_update_index_in_dim(out, value, place, 0)
    for step in range(1, count):
        got = lax.ppermute(value, axis_name, pairs_of(step))
        out = lax.dynamic_update_index_in_dim(out, got, (place - step) % count, 0)
    return out


def scatter_steps(value, axis_name, pairs_of, place, count):
    total = lax.dynamic_index_in_dim(value, place, 0, keepdims=False).astype(f32)
    for step in range(1, count):
        block = lax.dynamic_index_in_dim(value, (place + step) % count, 0, keepdims=False)
        total = total + lax.ppermute(block, axis_name, pairs_of(step)).astype(f32)
    return total


def sum_everywhere(value, sizes):
    for axis_name in ("shard", "seq", "dp"):
        bit = 1
        while bit < sizes[axis_name]:
            value = value + lax.ppermute(
                value, axis_name, [(i, i ^ bit) for i in range(sizes[axis_name])]
            )
            bit *= 2
    return value


def causal_blocks(seq_length):
    block_rows = min(512, seq_length)
    return [(start, start + block_rows) for start in range(0, seq_length, block_rows)]


def attention_forward(query, key, value):
    length = query.shape[1]
    outs, sums = [], []
    for start, end in causal_blocks(length):
        raw = jnp.einsum(
            "hqd,hkd->hqk", query[:, start:end], key[:, :end], preferred_element_type=f32
        ) * (HDIM**-0.5)
        causal = (start + jnp.arange(end - start))[:, None] >= jnp.arange(end)[None, :]
        scores = jnp.where(causal[None], raw, -1e30)
        row_top = jnp.max(scores, axis=-1, keepdims=True)
        row_total = jnp.sum(jnp.exp(scores - row_top), axis=-1, keepdims=True)
        log_total = row_top + jnp.log(row_total)
        soft = jnp.exp(scores - log_total).astype(bf16)
        outs.append(jnp.einsum("hqk,hkd->hqd", soft, value[:, :end], preferred_element_type=f32))
        sums.append(log_total)
    return jnp.concatenate(outs, axis=1), jnp.concatenate(sums, axis=1)


def attention_backward(query, key, value, sums, dout):
    heads, length, width = query.shape
    dqs = []
    dkey = jnp.zeros((heads, length, width), f32)
    dvalue = jnp.zeros((heads, length, width), f32)
    for start, end in causal_blocks(length):
        raw = jnp.einsum(
            "hqd,hkd->hqk", query[:, start:end], key[:, :end], preferred_element_type=f32
        ) * (HDIM**-0.5)
        causal = (start + jnp.arange(end - start))[:, None] >= jnp.arange(end)[None, :]
        scores = jnp.where(causal[None], raw, -1e30)
        soft = jnp.exp(scores - sums[:, start:end])
        dsoft = jnp.einsum(
            "hqd,hkd->hqk", dout[:, start:end], value[:, :end], preferred_element_type=f32
        )
        delta = jnp.sum(soft * dsoft, axis=-1, keepdims=True)
        dscores = (soft * (dsoft - delta)).astype(bf16)
        dqs.append(
            jnp.einsum("hqk,hkd->hqd", dscores, key[:, :end], preferred_element_type=f32)
            * (HDIM**-0.5)
        )
        dkey = dkey.at[:, :end].add(
            jnp.einsum("hqk,hqd->hkd", dscores, query[:, start:end], preferred_element_type=f32)
            * (HDIM**-0.5)
        )
        dvalue = dvalue.at[:, :end].add(
            jnp.einsum(
                "hqk,hqd->hkd", soft.astype(bf16), dout[:, start:end], preferred_element_type=f32
            )
        )
    return jnp.concatenate(dqs, axis=1), dkey, dvalue


def heads_first(value, heads):
    length = value.shape[0]
    return value.reshape(length, heads, HDIM).transpose(1, 0, 2)


def heads_last(value):
    heads, length, width = value.shape
    return value.transpose(1, 0, 2).reshape(length, heads * width)


def make_shards(sizes):
    n_dp, n_seq, n_shard = sizes["dp"], sizes["seq"], sizes["shard"]
    n_x = n_shard // 2

    def shards(
        tokens,
        cotangent,
        previous_logits,
        routes,
        priority,
        attention_master,
        vector_master,
        expert_master,
        mixing_master,
        attention_first,
        vector_first,
        expert_first,
        mixing_first,
        attention_second,
        vector_second,
        expert_second,
        mixing_second,
    ):
        z, y, s = lax.axis_index("dp"), lax.axis_index("seq"), lax.axis_index("shard")
        x_place, core = s // 2, s % 2
        row_count, model_width = tokens.shape[1], tokens.shape[2]
        half_width = model_width // 2
        local_experts = expert_master.shape[0]
        spread = local_experts == n_seq
        ep_axes = ("seq", "shard") if spread else ("shard",)
        own_rows = attention_master.shape[1]

        expert_low = expert_master.astype(bf16)
        if spread:
            kept_low = lax.dynamic_index_in_dim(expert_low, y, 0, keepdims=False)
            sent_low = lax.dynamic_index_in_dim(expert_low, 1 - y, 0, keepdims=False)
            rows_low = in_order(kept_low, swap_seq(sent_low), y, 1)
            expert_use = lax.all_gather(rows_low, "dp", axis=1, tiled=True)
        else:
            expert_use = lax.all_gather(expert_low[0], ("dp", "seq"), axis=1, tiled=True)

        attention_low = attention_master.astype(bf16)
        vector_low = vector_master.astype(bf16).T
        vector_pad = 128 - vector_low.shape[1]

        def weight_pack(which):
            columns = lax.dynamic_slice_in_dim(attention_low[:3], which * half_width, half_width, 2)
            return jnp.concatenate(
                [columns[0], columns[1], columns[2], attention_low[3], jnp.pad(vector_low, ((0, 0), (0, vector_pad)))],
                axis=1,
            )

        packed = in_order(
            weight_pack(y)[None], swap_seq(weight_pack(1 - y))[None], y, 0
        )
        packed = gather_steps(packed, "dp", lambda k: pairs_dp(n_dp, k), z, n_dp)
        packed = gather_steps(packed, "shard", lambda k: pairs_x(n_shard, k), x_place, n_x)
        packed = in_order(
            packed[None], lax.ppermute(packed, "shard", pairs_core(n_shard))[None], core, 0
        )
        packed = packed.transpose(2, 3, 1, 0, 4, 5).reshape(model_width, -1)
        qkv_weight = packed[:, : 3 * half_width]
        out_weight = packed[:, 3 * half_width : 3 * half_width + model_width]
        vector_all = packed[:, 3 * half_width + model_width :][:, : 4 + NEXP].T

        route_rows = routes[0]
        order = priority[0, 0]
        capacity = 9 * row_count * TOP // (8 * NEXP)
        expert_ids = jnp.arange(NEXP)[None, :]
        hit_each = [route_rows[:, j : j + 1] == expert_ids for j in range(TOP)]
        hits = (hit_each[0] | hit_each[1]).astype(bf16)
        before = (order[None, :] < order[:, None]).astype(bf16)
        counts = dot_nn(before, hits)
        kept, dispatch = [], []
        block_ids = jnp.arange(NFFN * capacity)[None, :]
        for j in range(TOP):
            slot = jnp.sum(jnp.where(hit_each[j], counts, 0.0), axis=1, keepdims=True).astype(
                jnp.int32
            )
            route = route_rows[:, j : j + 1]
            keep = (route < NFFN) & (slot < capacity)
            block = (route % n_seq) * n_shard + route // n_seq if spread else route
            kept.append(keep)
            dispatch.append(
                ((block_ids == block * capacity + slot) & keep).astype(bf16)
            )
        dispatch_both = dispatch[0] + dispatch[1]

        upstream = cotangent[0].astype(f32)
        dout_rows = dot_tn(dispatch_both, cotangent[0]).astype(bf16)
        dout_rows = lax.all_to_all(
            dout_rows.reshape(NFFN, capacity, model_width), ep_axes, 0, 0, tiled=True
        ).reshape(NFFN * capacity, model_width)

        tokens_other = swap_seq(tokens[0])
        tokens_all = in_order(tokens[0], tokens_other, y, 0).astype(f32)
        seq_length = tokens_all.shape[0]
        local_heads = HEADS // n_seq
        gain_one = vector_all[0].astype(f32)[None, :]
        gain_two = vector_all[1].astype(f32)[None, :]
        rho_all = lax.rsqrt(jnp.mean(tokens_all * tokens_all, axis=-1, keepdims=True) + norm_eps)
        normed = (tokens_all * rho_all * gain_one).astype(bf16)
        cosine, sine_table = rotary_tables(jnp.arange(seq_length).astype(f32))
        qkv = dot_nn(normed, qkv_weight)
        query = rotate(qkv[:, :half_width].reshape(seq_length, local_heads, HDIM), cosine, sine_table)
        key = rotate(
            qkv[:, half_width : 2 * half_width].reshape(seq_length, local_heads, HDIM),
            cosine,
            sine_table,
        )
        query = query.astype(bf16).transpose(1, 0, 2)
        key = key.astype(bf16).transpose(1, 0, 2)
        value = heads_first(qkv[:, 2 * half_width :].astype(bf16), local_heads)
        mixed, log_sums = attention_forward(query, key, value)
        mixed = heads_last(mixed.astype(bf16))
        mixed_keep = lax.dynamic_slice_in_dim(mixed, y * row_count, row_count, 0)
        mixed_send = lax.dynamic_slice_in_dim(mixed, (1 - y) * row_count, row_count, 0)
        mixed_tokens = in_order(mixed_keep, swap_seq(mixed_send), y, 1)

        inputs = tokens[0].astype(f32)
        resid = inputs + dot_nn(mixed_tokens, out_weight)
        rho_two = lax.rsqrt(jnp.mean(resid * resid, axis=-1, keepdims=True) + norm_eps)
        normed_two = resid * rho_two * gain_two
        expert_in = normed_two.astype(bf16)
        router = vector_all[4:]
        previous = previous_logits[0]
        logits = dot_nt(expert_in, router) + exact_dot(previous, mixing_master)
        gates = softmax_rows(logits)
        picked = [
            jnp.sum(jnp.where(hit_each[j], gates, 0.0), axis=1, keepdims=True) for j in range(TOP)
        ]

        taken = dot_tn(dispatch_both, expert_in).astype(bf16)
        taken = lax.all_to_all(
            taken.reshape(NFFN, capacity, model_width), ep_axes, 0, 0, tiled=True
        ).reshape(NFFN * capacity, model_width)
        gate_rows = (
            exact_dot(dispatch[0].astype(f32).T, picked[0])
            + exact_dot(dispatch[1].astype(f32).T, picked[1])
        ).reshape(NFFN, capacity)
        gate_rows = lax.all_to_all(gate_rows, ep_axes, 0, 0, tiled=True).reshape(
            NFFN * capacity, 1
        )

        gate_pre = dot_nn(taken, expert_use[0])
        up_pre = dot_nn(taken, expert_use[1])
        sig = jax.nn.sigmoid(gate_pre)
        hidden = (gate_pre * sig * up_pre).astype(bf16)
        result = dot_nt(hidden, expert_use[2]).astype(bf16)
        result = lax.all_to_all(
            result.reshape(NFFN, capacity, model_width), ep_axes, 0, 0, tiled=True
        ).reshape(NFFN * capacity, model_width)
        dresult = (gate_rows * dout_rows.astype(f32)).astype(bf16)
        dhidden = dot_nn(dresult, expert_use[2])
        dgate_low = (dhidden * up_pre * sig * (1.0 + gate_pre * (1.0 - sig))).astype(bf16)
        dup_low = (dhidden * gate_pre * sig).astype(bf16)
        dtaken = (dot_nt(dgate_low, expert_use[0]) + dot_nt(dup_low, expert_use[1])).astype(bf16)
        dtaken = lax.all_to_all(
            dtaken.reshape(NFFN, capacity, model_width), ep_axes, 0, 0, tiled=True
        ).reshape(NFFN * capacity, model_width)
        dexpert = jnp.stack(
            [
                dot_tn(taken, dgate_low).astype(bf16),
                dot_tn(taken, dup_low).astype(bf16),
                dot_tn(dresult, hidden).astype(bf16),
            ]
        )
        if spread:
            dexpert = lax.psum_scatter(dexpert, "dp", scatter_dimension=1, tiled=True)
            dexpert = dexpert.reshape(3, n_seq, -1, dexpert.shape[2])
            kept_part = lax.dynamic_index_in_dim(dexpert, y, 1, keepdims=False)
            sent_part = lax.dynamic_index_in_dim(dexpert, 1 - y, 1, keepdims=False)
            expert_sum = in_order(kept_part[None], swap_seq(sent_part)[None], y, 0)
        else:
            expert_sum = lax.psum_scatter(
                dexpert, ("dp", "seq"), scatter_dimension=1, tiled=True
            )[None]
        expert_sum = expert_sum.astype(f32)

        consts = vector_all[2:4].astype(f32)
        chosen = []
        for j in range(TOP):
            route = route_rows[:, j : j + 1]
            entry = dot_nn(dispatch[j], result) + jnp.where(route == NFFN + 1, normed_two, 0.0)
            entry = entry + jnp.where(route == NFFN + 2, consts[0:1], 0.0)
            entry = entry + jnp.where(route == NFFN + 3, consts[1:2], 0.0)
            chosen.append(entry)
        block_output = (resid + picked[0] * chosen[0] + picked[1] * chosen[1]).astype(bf16)
        dgates = jnp.zeros_like(gates)
        dnormed_two = dot_nn(dispatch_both, dtaken)
        dconst_one = jnp.zeros((1, model_width), f32)
        dconst_two = jnp.zeros((1, model_width), f32)
        for j in range(TOP):
            route = route_rows[:, j : j + 1]
            dpicked = jnp.sum(upstream * chosen[j], axis=-1, keepdims=True)
            dgates = dgates + jnp.where(hit_each[j], dpicked, 0.0)
            dvalue = picked[j] * upstream
            dnormed_two = dnormed_two + jnp.where(route == NFFN + 1, dvalue, 0.0)
            dconst_one = dconst_one + jnp.sum(
                jnp.where(route == NFFN + 2, dvalue, 0.0), axis=0, keepdims=True
            )
            dconst_two = dconst_two + jnp.sum(
                jnp.where(route == NFFN + 3, dvalue, 0.0), axis=0, keepdims=True
            )
        dlogits = gates * (dgates - jnp.sum(gates * dgates, axis=-1, keepdims=True))
        dnormed_two = dnormed_two + exact_dot(dlogits, router.astype(f32))
        drouter = exact_dot(dlogits.T, expert_in.astype(f32))
        dmixing = exact_dot(previous.T, dlogits)
        scaled_two = dnormed_two * gain_two
        dresid = upstream + (
            rho_two * scaled_two
            - resid * (rho_two * rho_two * rho_two) * jnp.mean(resid * scaled_two, -1, keepdims=True)
        )
        dgain_two = jnp.sum(dnormed_two * resid * rho_two, axis=0, keepdims=True)
        dbranch_low = dresid.astype(bf16)
        dweight_out = dot_tn(mixed_tokens, dbranch_low)
        dout_sum = lax.psum_scatter(
            dweight_out, ("dp", "seq", "shard"), scatter_dimension=0, tiled=True
        )
        dmixed = dot_nt(dbranch_low, out_weight).astype(bf16)
        dmixed_keep = lax.dynamic_slice_in_dim(dmixed, y * half_width, half_width, 1)
        dmixed_send = lax.dynamic_slice_in_dim(dmixed, (1 - y) * half_width, half_width, 1)
        dmixed_heads = heads_first(in_order(dmixed_keep, swap_seq(dmixed_send), y, 0), local_heads)

        dquery, dkey, dvalue_heads = attention_backward(query, key, value, log_sums, dmixed_heads)
        dquery = dquery.astype(bf16).astype(f32).transpose(1, 0, 2)
        dkey = dkey.astype(bf16).astype(f32).transpose(1, 0, 2)
        dqkv = jnp.concatenate(
            [
                rotate_back(dquery, cosine, sine_table).astype(bf16).reshape(seq_length, -1),
                rotate_back(dkey, cosine, sine_table).astype(bf16).reshape(seq_length, -1),
                heads_last(dvalue_heads.astype(bf16)),
            ],
            axis=1,
        )
        dnormed_all = dot_nt(dqkv, qkv_weight)
        dnormed_keep = lax.dynamic_slice_in_dim(dnormed_all, y * row_count, row_count, 0)
        dnormed_send = lax.dynamic_slice_in_dim(dnormed_all, (1 - y) * row_count, row_count, 0)
        dnormed = dnormed_keep + swap_seq(dnormed_send.astype(bf16)).astype(f32)
        rho_one = lax.rsqrt(jnp.mean(inputs * inputs, axis=-1, keepdims=True) + norm_eps)
        scaled_one = dnormed * gain_one
        input_gradient = dresid + (
            rho_one * scaled_one
            - inputs * (rho_one * rho_one * rho_one) * jnp.mean(inputs * scaled_one, -1, keepdims=True)
        )
        dgain_one = jnp.sum(dnormed * inputs * rho_one, axis=0, keepdims=True)

        dweight_qkv = dot_tn(normed, dqkv)
        dvector = jnp.concatenate([dgain_one, dgain_two, dconst_one, dconst_two, drouter], axis=0)
        dpack = jnp.concatenate(
            [dweight_qkv, jnp.pad(dvector.T, ((0, 0), (0, vector_pad)))], axis=1
        )
        columns = dpack.shape[1]
        dpack = dpack.reshape(n_dp, n_seq, n_x, 2, own_rows, columns).transpose(3, 2, 0, 1, 4, 5)
        core_keep = lax.dynamic_index_in_dim(dpack, core, 0, keepdims=False)
        core_send = lax.dynamic_index_in_dim(dpack, 1 - core, 0, keepdims=False)
        dpack = core_keep + lax.ppermute(core_send, "shard", pairs_core(n_shard))
        dpack = scatter_steps(
            dpack.astype(bf16), "shard", lambda k: pairs_x(n_shard, k), x_place, n_x
        )
        dpack = scatter_steps(dpack.astype(bf16), "dp", lambda k: pairs_dp(n_dp, k), z, n_dp)
        part_keep = lax.dynamic_index_in_dim(dpack, y, 0, keepdims=False)
        part_send = lax.dynamic_index_in_dim(dpack, 1 - y, 0, keepdims=False)
        part_got = swap_seq(part_send)
        qkv_both = in_order(
            part_keep[:, : 3 * half_width].reshape(own_rows, 3, half_width),
            part_got[:, : 3 * half_width].reshape(own_rows, 3, half_width),
            y,
            2,
        ).transpose(1, 0, 2)
        attention_sum = jnp.concatenate([qkv_both, dout_sum[None]], axis=0)
        vector_sum = (part_keep + part_got)[:, 3 * half_width : 3 * half_width + 4 + NEXP].T

        attention_m, attention_s, attention_u = moments(
            attention_master, attention_first, attention_second, attention_sum
        )
        vector_m, vector_s, vector_u = moments(
            vector_master, vector_first, vector_second, vector_sum
        )
        expert_m, expert_s, expert_u = moments(
            expert_master, expert_first, expert_second, expert_sum
        )

        def squares(attention_x, vector_x, expert_x):
            vector_parts = jnp.sum(vector_x * vector_x, axis=1)
            expert_parts = lax.dynamic_update_slice_in_dim(
                jnp.zeros((NFFN * 3,), f32),
                jnp.sum(expert_x * expert_x, axis=(2, 3)).reshape(-1),
                s * local_experts * 3,
                0,
            )
            return jnp.concatenate(
                [
                    jnp.sum(attention_x * attention_x, axis=(1, 2)),
                    vector_parts[0:2],
                    jnp.sum(vector_parts[2:4])[None],
                    jnp.sum(vector_parts[4:])[None],
                    expert_parts,
                ]
            )

        count = 8 + 3 * NFFN
        small = jnp.concatenate(
            [
                squares(attention_master, vector_master, expert_master),
                squares(attention_u, vector_u, expert_u),
                dmixing.reshape(-1),
            ]
        )
        used = small.shape[0]
        small = jnp.pad(small, (0, -used % 128)).reshape(-1, 128)
        small = sum_everywhere(small, sizes).reshape(-1)
        summed_squares = small[: 2 * count].reshape(2, count)
        mixing_grad = small[2 * count : used].reshape(NEXP, NEXP)
        mixing_m, mixing_s, mixing_u = moments(
            mixing_master, mixing_first, mixing_second, mixing_grad
        )
        mixing_squares = jnp.stack(
            [jnp.sum(mixing_master * mixing_master), jnp.sum(mixing_u * mixing_u)]
        )
        tensor_norms = jnp.sqrt(jnp.concatenate([summed_squares, mixing_squares[:, None]], axis=1))
        ratios = learn_rate * (tensor_norms[0] / (tensor_norms[1] + norm_eps))
        vector_ratio = jnp.concatenate(
            [
                ratios[4:6],
                jnp.broadcast_to(ratios[6:7], (2,)),
                jnp.broadcast_to(ratios[7:8], (NEXP,)),
            ]
        )[:, None]
        expert_ratio = lax.dynamic_slice_in_dim(
            ratios[8:count].reshape(NFFN, 3), s * local_experts, local_experts, 0
        )[:, :, None, None]
        return (
            block_output[None],
            input_gradient[None],
            attention_master - ratios[0:4][:, None, None] * attention_u,
            vector_master - vector_ratio * vector_u,
            expert_master - expert_ratio * expert_u,
            mixing_master - ratios[count] * mixing_u,
            attention_m,
            vector_m,
            expert_m,
            mixing_m,
            attention_s,
            vector_s,
            expert_s,
            mixing_s,
            tensor_norms,
        )

    return shards


def solution(mesh):
    tokens_spec = P(("dp", "shard"), "seq", None)
    attention_spec = P(None, ("dp", "seq", "shard"), None)
    vector_spec = P(None, ("dp", "seq", "shard"))
    expert_spec = P("shard", None, ("dp", "seq"), None)
    weights = (attention_spec, vector_spec, expert_spec, P())
    return jax.shard_map(
        make_shards(dict(mesh.shape)),
        mesh=mesh,
        in_specs=(tokens_spec,) * 5 + weights * 3,
        out_specs=(tokens_spec,) * 2 + weights * 3 + (P(),),
        check_vma=False,
    )
```

```python
import jax
import jax.numpy as jnp
from jax import lax
from jax.experimental import pallas as pl
from jax.experimental.pallas import tpu as pltpu
from jax.sharding import PartitionSpec as P

HEADS = 12
HDIM = 64
NFFN = 8
TOP = 2
STEP = 4
NEXP = 12

beta_one = 0.9
beta_two = 0.999
adam_eps = 1e-06
weight_decay = 0.01
learn_rate = 0.25
norm_eps = 1e-06
rope_base = 10000.0

bf16 = jnp.bfloat16
f32 = jnp.float32


def exact_dot(left, right):
    return jnp.dot(left, right, precision=lax.Precision.HIGHEST, preferred_element_type=f32)


def dot_nn(left, right):
    return lax.dot_general(left, right, (((1,), (0,)), ((), ())), preferred_element_type=f32)


def dot_nt(left, right):
    return lax.dot_general(left, right, (((1,), (1,)), ((), ())), preferred_element_type=f32)


def dot_tn(left, right):
    return lax.dot_general(left, right, (((0,), (0,)), ((), ())), preferred_element_type=f32)


def rotary_tables(length):
    freqs = rope_base ** (-jnp.arange(0, HDIM, 2).astype(f32) / HDIM)
    angles = jnp.arange(length).astype(f32)[:, None] * freqs[None, :]
    cosine, sine = jnp.cos(angles), jnp.sin(angles)
    return (
        jnp.concatenate([cosine] * 4, axis=-1),
        jnp.concatenate([-sine, sine, -sine, sine], axis=-1),
    )


def softmax_rows(logits):
    row_top = jnp.max(logits, axis=-1, keepdims=True)
    expd_values = jnp.exp(logits - row_top)
    return expd_values / jnp.sum(expd_values, axis=-1, keepdims=True)


def moments(weight, first, second, grad):
    first_new = beta_one * first + (1.0 - beta_one) * grad
    second_new = beta_two * second + (1.0 - beta_two) * grad * grad
    step_value = (
        first_new
        / (1.0 - beta_one**STEP)
        / (jnp.sqrt(second_new / (1.0 - beta_two**STEP)) + adam_eps)
        + weight_decay * weight
    )
    return (first_new, second_new, step_value)


DP = ("dp_far", "dp_near")
SHARD = ("x", "core")


def after(value, *others):
    return lax.optimization_barrier((value,) + others)[0]


def swap(value, axis_name):
    return lax.ppermute(value, axis_name, [(0, 1), (1, 0)])


def swap_seq(value):
    return swap(value, "seq")


def in_order(own, other, which, axis):
    low = jnp.where(which == 0, own, other)
    high = jnp.where(which == 0, other, own)
    return jnp.concatenate([low, high], axis=axis)


def gather_steps(value, axis_name, place, count):
    out = jnp.zeros((count,) + value.shape, value.dtype)
    out = lax.dynamic_update_index_in_dim(out, value, place, 0)
    for step in range(1, count):
        got = lax.ppermute(value, axis_name, [(i, (i + step) % count) for i in range(count)])
        out = lax.dynamic_update_index_in_dim(out, got, (place - step) % count, 0)
    return out


def scatter_steps(value, axis_name, place, count):
    total = lax.dynamic_index_in_dim(value, place, 0, keepdims=False).astype(f32)
    for step in range(1, count):
        block = lax.dynamic_index_in_dim(value, (place + step) % count, 0, keepdims=False)
        got = lax.ppermute(block, axis_name, [(i, (i + step) % count) for i in range(count)])
        total = total + got.astype(f32)
    return total


def keep_and_send(value, place, axis):
    return (
        lax.dynamic_index_in_dim(value, place, axis, keepdims=False),
        lax.dynamic_index_in_dim(value, 1 - place, axis, keepdims=False),
    )


def sum_everywhere(value, sizes):
    for axis_name in ("core", "x", "seq", "dp_near", "dp_far"):
        bit = 1
        while bit < sizes[axis_name]:
            value = value + lax.ppermute(
                value, axis_name, [(i, i ^ bit) for i in range(sizes[axis_name])]
            )
            bit *= 2
    return value


QUERY_ROWS = 256
FF_COLUMNS = 512

def turn(value):
    lane = lax.broadcasted_iota(jnp.int32, value.shape, 1) % HDIM
    return jnp.where(lane < HDIM // 2, pltpu.roll(value, 96, 1), pltpu.roll(value, 32, 1))

def attention_forward_kernel(x_ref, gain_ref, wq_ref, wk_ref, wv_ref, cos_ref, sin_ref, h_ref, q_ref, k_ref, v_ref, o_ref, lse_ref):
    length = x_ref.shape[0]

    @pl.when(pl.program_id(0) == 0)
    def _():
        for start in range(0, length, QUERY_ROWS):
            rows = pl.ds(start, QUERY_ROWS)
            x = x_ref[rows, :].astype(f32)
            rho = lax.rsqrt(jnp.mean(x * x, axis=-1, keepdims=True) + norm_eps)
            h_ref[rows, :] = (x * rho * gain_ref[...]).astype(bf16)

    for start in range(0, length, QUERY_ROWS):
        rows = pl.ds(start, QUERY_ROWS)
        h = h_ref[rows, :]
        cos, sin = cos_ref[rows, :], sin_ref[rows, :]
        q = dot_nn(h, wq_ref[...])
        k = dot_nn(h, wk_ref[...])
        q_ref[rows, :] = (q * cos + turn(q) * sin).astype(bf16)
        k_ref[rows, :] = (k * cos + turn(k) * sin).astype(bf16)
        v_ref[rows, :] = dot_nn(h, wv_ref[...]).astype(bf16)

    ahead = lax.broadcasted_iota(jnp.int32, (QUERY_ROWS, QUERY_ROWS), 1) > lax.broadcasted_iota(jnp.int32, (QUERY_ROWS, QUERY_ROWS), 0)
    for start in range(0, length, QUERY_ROWS):
        end = start + QUERY_ROWS
        outs = []
        for head in range(2):
            lanes = slice(head * HDIM, (head + 1) * HDIM)
            q = q_ref[start:end, lanes]
            s = dot_nt(q, k_ref[:end, lanes]) * (HDIM**-0.5)
            last = jnp.where(ahead, -1e30, s[:, start:])
            s = jnp.concatenate([s[:, :start], last], axis=1) if start else last
            top = jnp.max(s, axis=-1, keepdims=True)
            p = jnp.exp(s - top)
            total = jnp.sum(p, axis=-1, keepdims=True)
            p = (p * (1.0 / total)).astype(bf16)
            outs.append(dot_nn(p, v_ref[:end, lanes]))
            lse = jnp.broadcast_to(top + jnp.log(total), (QUERY_ROWS, 128))
            lse_ref[0, head : head + 1, start:end] = lse.T[0:1, :]
        o_ref[start:end, :] = jnp.concatenate(outs, axis=1).astype(bf16)

def attention_forward(x, gain, weight, cos, sin):
    length, width = x.shape
    half = weight.shape[1] // 3
    pairs = half // 128
    full = lambda shape: pl.BlockSpec(shape, lambda p: (0,) * len(shape))
    col = lambda base: pl.BlockSpec((width, 128), lambda p, base=base: (0, base + p))
    out_col = pl.BlockSpec((length, 128), lambda p: (0, p))
    return pl.pallas_call(
        attention_forward_kernel,
        grid=(pairs,),
        in_specs=[full((length, width)), full((1, width)), col(0), col(pairs), col(2 * pairs), full((length, 128)), full((length, 128))],
        out_specs=[full((length, width)), out_col, out_col, out_col, out_col, pl.BlockSpec((1, 2, length), lambda p: (p, 0, 0))],
        out_shape=[jax.ShapeDtypeStruct((length, width), bf16)] + [jax.ShapeDtypeStruct((length, half), bf16)] * 4 + [jax.ShapeDtypeStruct((pairs, 2, length), f32)],
        compiler_params=pltpu.CompilerParams(vmem_limit_bytes=40 * 2**20),
        cost_estimate=pl.CostEstimate(flops=6 * length * width * half + 4 * length * length * half, bytes_accessed=8 * length * width, transcendentals=length * length * half // HDIM),
    )(x, gain, weight, weight, weight, cos, sin)

def attention_backward_kernel(h_ref, q_ref, k_ref, v_ref, do_ref, lse_ref, wq_ref, wk_ref, wv_ref, cos_ref, sin_ref, dw_ref, dh_ref, dq_scr, dk_scr, dv_scr):
    length = h_ref.shape[0]
    step = pl.program_id(0)
    behind = lax.broadcasted_iota(jnp.int32, (QUERY_ROWS, QUERY_ROWS), 0) > lax.broadcasted_iota(jnp.int32, (QUERY_ROWS, QUERY_ROWS), 1)
    dk_scr[...] = jnp.zeros_like(dk_scr)
    dv_scr[...] = jnp.zeros_like(dv_scr)
    for start in range(0, length, QUERY_ROWS):
        end = start + QUERY_ROWS
        for head in range(2):
            lanes = slice(head * HDIM, (head + 1) * HDIM)
            q, do = q_ref[start:end, lanes], do_ref[start:end, lanes]
            k, v = k_ref[:end, lanes], v_ref[:end, lanes]
            s = dot_nt(k, q) * (HDIM**-0.5) - lse_ref[0, head : head + 1, start:end]
            last = jnp.where(behind, -1e30, s[start:])
            s = jnp.concatenate([s[:start], last], axis=0) if start else last
            p = jnp.exp(s)
            dp = dot_nt(v, do)
            delta = jnp.sum(p * dp, axis=0, keepdims=True)
            ds = (p * (dp - delta)).astype(bf16)
            dq_scr[start:end, lanes] = dot_tn(ds, k) * (HDIM**-0.5)
            dk_scr[:end, lanes] += dot_nn(ds, q)
            dv_scr[:end, lanes] += dot_nn(p.astype(bf16), do)
    cos, sin = cos_ref[...], sin_ref[...]

    dq = dq_scr[...].astype(bf16).astype(f32)
    dk = (dk_scr[...] * (HDIM**-0.5)).astype(bf16).astype(f32)
    dqp = (dq * cos + turn(dq * sin)).astype(bf16)
    dkp = (dk * cos + turn(dk * sin)).astype(bf16)
    dvb = dv_scr[...].astype(bf16)
    d = jnp.concatenate([dqp, dkp, dvb], axis=1)
    w = jnp.concatenate([wq_ref[...], wk_ref[...], wv_ref[...]], axis=1)
    dw_ref[...] = dot_tn(h_ref[...], d).astype(bf16)
    dh = dot_nt(d, w)

    @pl.when(step == 0)
    def _():
        dh_ref[...] = dh

    @pl.when(step > 0)
    def _():
        dh_ref[...] += dh

def attention_backward(h, q, k, v, do, lse, weight, cos, sin):
    length, width = h.shape
    half = weight.shape[1] // 3
    pairs = half // 128
    full = lambda shape: pl.BlockSpec(shape, lambda p: (0,) * len(shape))
    col = lambda base: pl.BlockSpec((width, 128), lambda p, base=base: (0, base + p))
    out_col = pl.BlockSpec((length, 128), lambda p: (0, p))
    return pl.pallas_call(
        attention_backward_kernel,
        grid=(pairs,),
        in_specs=[full((length, width)), out_col, out_col, out_col, out_col, pl.BlockSpec((1, 2, length), lambda p: (p, 0, 0)), col(0), col(pairs), col(2 * pairs), full((length, 128)), full((length, 128))],
        out_specs=[pl.BlockSpec((width, 384), lambda p: (0, p)), full((length, width))],
        out_shape=[jax.ShapeDtypeStruct((width, 3 * half), bf16), jax.ShapeDtypeStruct((length, width), f32)],
        scratch_shapes=[pltpu.VMEM((length, 128), f32)] * 3,
        compiler_params=pltpu.CompilerParams(vmem_limit_bytes=48 * 2**20),
        cost_estimate=pl.CostEstimate(flops=12 * length * width * half + 10 * length * length * half, bytes_accessed=12 * length * width, transcendentals=length * length * half // HDIM),
    )(h, q, k, v, do, lse, weight, weight, weight, cos, sin)


def three_parts(value):
    high = value.astype(bf16)
    rest = value - high.astype(f32)
    middle = rest.astype(bf16)
    low = (rest - middle.astype(f32)).astype(bf16)
    lane = lax.broadcasted_iota(jnp.int32, (value.shape[0], 128), 1)
    zero = jnp.zeros((), bf16)
    return jnp.where(lane == 0, high, jnp.where(lane == 1, middle, jnp.where(lane == 2, low, zero)))

def three_parts_rounded(value):
    high = lax.reduce_precision(value, 8, 7)
    middle = lax.reduce_precision(value - high, 8, 7)
    low = lax.reduce_precision(value - high - middle, 8, 7)
    lane = lax.broadcasted_iota(jnp.int32, (value.shape[0], 128), 1)
    return (
        jnp.where(lane == 0, high, 0.0)
        + jnp.where(lane == 1, middle, 0.0)
        + jnp.where(lane == 2, low, 0.0)
    ).astype(bf16)


def expert_kernel(taken_ref, dout_ref, weight_ref, f_ref, dtaken_ref, hidden_ref, dgate_ref, dup_ref, dresult_ref, f_acc, d_acc):
    step, last = pl.program_id(0), pl.num_programs(0) - 1
    width = dout_ref.shape[1]

    @pl.when(step == 0)
    def _():
        parts = taken_ref[:, width:].astype(f32)
        gate = jnp.sum(parts, axis=1, keepdims=True)
        dresult_ref[...] = (gate * dout_ref[...].astype(f32)).astype(bf16)
        f_acc[...] = jnp.zeros_like(f_acc)
        d_acc[...] = jnp.zeros_like(d_acc)

    taken = taken_ref[:, :width]
    a = dot_nn(taken, weight_ref[0])
    b = dot_nn(taken, weight_ref[1])
    sig = jax.nn.sigmoid(a)
    act = a * sig
    hidden = (act * b).astype(bf16)
    hidden_ref[...] = hidden
    f_acc[...] += dot_nt(hidden, weight_ref[2])
    dhidden = dot_nn(dresult_ref[...], weight_ref[2])
    dgate = (dhidden * b * (sig * (1.0 + a - act))).astype(bf16)
    dup = (dhidden * act).astype(bf16)
    dgate_ref[...] = dgate
    dup_ref[...] = dup
    d_acc[...] += dot_nt(dgate, weight_ref[0]) + dot_nt(dup, weight_ref[1])

    @pl.when(step == last)
    def _():
        f = f_acc[...].astype(bf16)
        f_ref[...] = f
        dtaken_ref[:, :width] = d_acc[...].astype(bf16)
        dpicked = jnp.sum(dout_ref[...].astype(f32) * f.astype(f32), axis=1, keepdims=True)
        dtaken_ref[:, width:] = three_parts(dpicked)

def expert_compute(taken, dout, weight):
    rows, width = dout.shape
    hidden = weight.shape[2]
    whole = lambda columns: pl.BlockSpec((rows, columns), lambda i: (0, 0))
    part = pl.BlockSpec((rows, FF_COLUMNS), lambda i: (0, i))
    shape = lambda columns: jax.ShapeDtypeStruct((rows, columns), bf16)
    return pl.pallas_call(
        expert_kernel,
        grid=(hidden // FF_COLUMNS,),
        in_specs=[whole(width + 128), whole(width), pl.BlockSpec((3, width, FF_COLUMNS), lambda i: (0, 0, i))],
        out_specs=[whole(width), whole(width + 128), part, part, part, whole(width)],
        out_shape=[shape(width), shape(width + 128), shape(hidden), shape(hidden), shape(hidden), shape(width)],
        scratch_shapes=[pltpu.VMEM((rows, width), f32)] * 2,
        compiler_params=pltpu.CompilerParams(vmem_limit_bytes=48 * 2**20),
        cost_estimate=pl.CostEstimate(flops=14 * rows * width * hidden, bytes_accessed=6 * width * hidden + 6 * rows * hidden, transcendentals=rows * hidden),
    )(taken, dout, weight)


def make_shards(sizes):
    n_seq, n_x = sizes["seq"], sizes["x"]
    n_dp = sizes["dp_far"] * sizes["dp_near"]

    def shards(
        tokens,
        cotangent,
        previous_logits,
        routes,
        priority,
        attention_master,
        vector_master,
        expert_master,
        mixing_master,
        attention_first,
        vector_first,
        expert_first,
        mixing_first,
        attention_second,
        vector_second,
        expert_second,
        mixing_second,
    ):
        z, y, s = lax.axis_index(DP), lax.axis_index("seq"), lax.axis_index(SHARD)
        far, near = lax.axis_index("dp_far"), lax.axis_index("dp_near")
        x_place, core = lax.axis_index("x"), lax.axis_index("core")
        row_count, model_width = tokens.shape[1], tokens.shape[2]
        half_width = model_width // 2
        local_experts = expert_master.shape[0]
        spread = local_experts == 2 and n_x == 2 and sizes["dp_far"] == 2
        ep_axes = ("dp_near", "seq", "x") if spread else SHARD
        own_rows = attention_master.shape[1]

        def cross(same_y, other_y):
            got = lax.ppermute(same_y, ("dp_near", "core"), [(1, 2), (2, 1)])
            moves = [
                (4 * n + 2 * q + c, 4 * c + 2 * (1 - q) + n)
                for n in range(2)
                for q in range(2)
                for c in range(2)
            ]
            return (
                jnp.where(near == core, same_y, got),
                lax.ppermute(other_y, ("dp_near", "seq", "core"), moves),
            )

        attention_low = attention_master.astype(bf16)
        vector_low = vector_master.astype(bf16).T
        vector_pad = 128 - vector_low.shape[1]

        def weight_pack(which):
            columns = lax.dynamic_slice_in_dim(attention_low[:3], which * half_width, half_width, 2)
            return jnp.concatenate(
                [columns[0], columns[1], columns[2], attention_low[3], jnp.pad(vector_low, ((0, 0), (0, vector_pad)))],
                axis=1,
            )

        packed = in_order(weight_pack(y)[None], swap_seq(weight_pack(1 - y))[None], y, 0)
        packed_z = gather_steps(packed, DP, z, n_dp)

        expert_low = after(expert_master, packed).astype(bf16)
        if spread:
            rows_low = in_order(*cross(*keep_and_send(expert_low, y, 0)), y, 1)
            rows_low = after(rows_low, packed_z)
            expert_use = lax.all_gather(rows_low, ("dp_far", "core"), axis=1, tiled=True)
        else:
            rows_low = expert_low[0]
            expert_use = lax.all_gather(rows_low, DP + ("seq",), axis=1, tiled=True)

        packed = gather_steps(packed_z, "x", x_place, n_x)
        packed = in_order(packed[None], swap(packed, "core")[None], core, 0)
        packed = packed.transpose(2, 3, 1, 0, 4, 5).reshape(model_width, -1)
        qkv_weight = packed[:, : 3 * half_width]
        out_weight = packed[:, 3 * half_width : 3 * half_width + model_width]
        vector_all = packed[:, 3 * half_width + model_width :][:, : 4 + NEXP].T

        route_rows = routes[0]
        order = priority[0, 0]
        capacity = 9 * row_count * TOP // (8 * NEXP)
        expert_ids = jnp.arange(NEXP)[None, :]
        hit_each = [route_rows[:, j : j + 1] == expert_ids for j in range(TOP)]
        hits = (hit_each[0] | hit_each[1]).astype(bf16)
        before = (order[None, :] < order[:, None]).astype(bf16)
        counts = dot_nn(before, hits)
        kept, dispatch = [], []
        block_ids = jnp.arange(NFFN * capacity)[None, :]
        for j in range(TOP):
            slot = jnp.sum(jnp.where(hit_each[j], counts, 0.0), axis=1, keepdims=True).astype(
                jnp.int32
            )
            route = route_rows[:, j : j + 1]
            keep = (route < NFFN) & (slot < capacity)
            block = ((route // 2) % 2) * 4 + (route % 2) * 2 + route // 4 if spread else route
            kept.append(keep)
            dispatch.append(
                ((block_ids == block * capacity + slot) & keep).astype(bf16)
            )
        dispatch_both = dispatch[0] + dispatch[1]

        tokens_all = in_order(tokens[0], swap_seq(after(tokens[0], rows_low)), y, 0)
        gain_one = vector_all[0].astype(f32)[None, :]
        gain_two = vector_all[1].astype(f32)[None, :]
        cosine, sine = rotary_tables(tokens_all.shape[0])
        normed, query, key, value, mixed, log_sums = attention_forward(
            tokens_all, gain_one, qkv_weight, cosine, sine
        )

        upstream = cotangent[0].astype(f32)
        dout_rows = dot_tn(dispatch_both, after(cotangent[0], tokens_all)).astype(bf16)
        dout_rows = lax.all_to_all(
            dout_rows.reshape(NFFN, capacity, model_width), ep_axes, 0, 0, tiled=True
        ).reshape(NFFN * capacity, model_width)
        mixed, dout_rows = lax.optimization_barrier((mixed, dout_rows))

        mixed_keep = lax.dynamic_slice_in_dim(mixed, y * row_count, row_count, 0)
        mixed_send = lax.dynamic_slice_in_dim(mixed, (1 - y) * row_count, row_count, 0)
        mixed_tokens = in_order(mixed_keep, swap_seq(mixed_send), y, 1)

        inputs = tokens[0].astype(f32)
        resid = inputs + dot_nn(mixed_tokens, out_weight)
        rho_two = lax.rsqrt(jnp.mean(resid * resid, axis=-1, keepdims=True) + norm_eps)
        normed_two = resid * rho_two * gain_two
        expert_in = normed_two.astype(bf16)
        router = vector_all[4:]
        previous = previous_logits[0]
        logits = dot_nt(expert_in, router) + exact_dot(previous, mixing_master)
        gates = softmax_rows(logits)
        picked = [
            jnp.sum(jnp.where(hit_each[j], gates, 0.0), axis=1, keepdims=True) for j in range(TOP)
        ]

        consts = vector_all[2:4].astype(f32)
        dlocal = [
            jnp.sum(upstream * normed_two, axis=-1, keepdims=True),
            jnp.sum(upstream * consts[0:1], axis=-1, keepdims=True),
            jnp.sum(upstream * consts[1:2], axis=-1, keepdims=True),
        ]

        def to_experts(rows):
            rows = rows.reshape(NFFN, capacity, rows.shape[1])
            return lax.all_to_all(rows, ep_axes, 0, 0, tiled=True).reshape(NFFN * capacity, -1)

        gate_parts = [three_parts_rounded(picked[j]) for j in range(TOP)]
        taken = dot_tn(
            jnp.concatenate(dispatch, axis=0),
            jnp.concatenate(
                [jnp.concatenate([expert_in, gate_parts[j]], axis=1) for j in range(TOP)], axis=0
            ),
        ).astype(bf16)
        taken = to_experts(taken)
        result, dtaken, hidden, dgate_low, dup_low, dresult = expert_compute(
            taken, dout_rows, expert_use
        )
        dtaken = to_experts(dtaken)
        result = to_experts(after(result, dtaken))
        taken = taken[:, :model_width]

        def sum_rows(grad):
            if not spread:
                return lax.psum_scatter(grad, DP + ("seq",), scatter_dimension=0, tiled=True)[None]
            grad = lax.psum_scatter(grad, ("dp_far", "core"), scatter_dimension=0, tiled=True)
            grad = grad.reshape(2, -1, grad.shape[1])
            same_y, other_y = cross(*keep_and_send(grad, y, 0))
            return in_order(same_y[None], other_y[None], y, 0)

        hidden_width = hidden.shape[1]
        ddown = sum_rows(dot_tn(dresult, hidden).astype(bf16))
        dgate_up = sum_rows(dot_tn(taken, jnp.concatenate([dgate_low, dup_low], axis=1)).astype(bf16))
        expert_sum = jnp.stack(
            [dgate_up[..., :hidden_width], dgate_up[..., hidden_width:], ddown], axis=1
        ).astype(f32)

        dgates = jnp.zeros_like(gates)
        dnormed_two = dot_nn(dispatch_both, dtaken[:, :model_width])
        value_weight = [0.0, 0.0, 0.0]
        for j in range(TOP):
            route = route_rows[:, j : j + 1]
            local = [jnp.where(route == NFFN + 1 + i, 1.0, 0.0) for i in range(3)]
            parts = dot_nn(dispatch[j], dtaken[:, model_width:])
            dpicked = jnp.sum(parts, axis=1, keepdims=True)
            for i in range(3):
                dpicked = dpicked + jnp.where(route == NFFN + 1 + i, dlocal[i], 0.0)
                value_weight[i] = value_weight[i] + local[i] * picked[j]
            dgates = dgates + jnp.where(hit_each[j], dpicked, 0.0)
        dnormed_two = dnormed_two + value_weight[0] * upstream
        dconst_one = jnp.sum(value_weight[1] * upstream, axis=0, keepdims=True)
        dconst_two = jnp.sum(value_weight[2] * upstream, axis=0, keepdims=True)
        mixture = (
            picked[0] * dot_nn(dispatch[0], result)
            + picked[1] * dot_nn(dispatch[1], result)
            + value_weight[0] * normed_two
            + value_weight[1] * consts[0:1]
            + value_weight[2] * consts[1:2]
        )
        block_output = (resid + mixture).astype(bf16)
        dlogits = gates * (dgates - jnp.sum(gates * dgates, axis=-1, keepdims=True))
        dnormed_two = dnormed_two + exact_dot(dlogits, router.astype(f32))
        drouter = exact_dot(dlogits.T, expert_in.astype(f32))
        dmixing = exact_dot(previous.T, dlogits)
        scaled_two = dnormed_two * gain_two
        dresid = upstream + (
            rho_two * scaled_two
            - resid * (rho_two * rho_two * rho_two) * jnp.mean(resid * scaled_two, -1, keepdims=True)
        )
        dgain_two = jnp.sum(dnormed_two * resid * rho_two, axis=0, keepdims=True)
        dbranch_low = dresid.astype(bf16)
        dweight_out = dot_tn(mixed_tokens, dbranch_low)

        group, place = n_seq * n_x, y * n_x + x_place

        def core_sum(grad):
            grad = grad.astype(bf16).reshape(n_dp, n_seq, n_x, 2, own_rows, -1)
            keep, send = keep_and_send(grad.transpose(3, 1, 2, 0, 4, 5), core, 0)
            return (keep.astype(f32) + swap(send, "core").astype(f32)).astype(bf16)

        def plane_sum(grad):
            grad = grad.reshape((group,) + grad.shape[2:])
            totals = [lax.dynamic_index_in_dim(grad, place, 0, keepdims=False).astype(f32), 0.0]
            for step in range(1, group):
                block = lax.dynamic_index_in_dim(grad, place ^ step, 0, keepdims=False)
                got = lax.ppermute(block, ("seq", "x"), [(i, i ^ step) for i in range(group)])
                totals[step // n_x] = totals[step // n_x] + got.astype(f32)
            return totals

        def dp_sum(grad):
            return scatter_steps(grad.astype(bf16), DP, z, n_dp)

        dout_part = core_sum(dweight_out)
        dmixed = dot_nt(dbranch_low, out_weight).astype(bf16)
        dmixed_keep = lax.dynamic_slice_in_dim(dmixed, y * half_width, half_width, 1)
        dmixed_send = lax.dynamic_slice_in_dim(dmixed, (1 - y) * half_width, half_width, 1)
        dmixed_heads = in_order(dmixed_keep, swap_seq(dmixed_send), y, 0)
        dmixed_heads = after(dmixed_heads, dout_part)
        dweight_qkv, dnormed_all = attention_backward(
            normed, query, key, value, dmixed_heads, log_sums, qkv_weight, cosine, sine
        )
        dout_sum = dp_sum(sum(plane_sum(dout_part)))
        dnormed_keep = lax.dynamic_slice_in_dim(dnormed_all, y * row_count, row_count, 0)
        dnormed_send = lax.dynamic_slice_in_dim(dnormed_all, (1 - y) * row_count, row_count, 0)
        dnormed = dnormed_keep + swap_seq(dnormed_send.astype(bf16)).astype(f32)
        rho_one = lax.rsqrt(jnp.mean(inputs * inputs, axis=-1, keepdims=True) + norm_eps)
        scaled_one = dnormed * gain_one
        input_gradient = dresid + (
            rho_one * scaled_one
            - inputs * (rho_one * rho_one * rho_one) * jnp.mean(inputs * scaled_one, -1, keepdims=True)
        )
        dgain_one = jnp.sum(dnormed * inputs * rho_one, axis=0, keepdims=True)

        dvector = jnp.concatenate([dgain_one, dgain_two, dconst_one, dconst_two, drouter], axis=0)
        qkv_part = core_sum(dweight_qkv)
        vector_part = core_sum(jnp.pad(dvector.T, ((0, 0), (0, vector_pad))))
        this_y, other_y = plane_sum(jnp.concatenate([qkv_part, vector_part], axis=-1))
        columns = 3 * half_width
        dpack = dp_sum(
            jnp.concatenate(
                [
                    this_y[..., :columns],
                    other_y[..., :columns],
                    this_y[..., columns:] + other_y[..., columns:],
                ],
                axis=-1,
            )
        )
        head_pairs = half_width // 128

        def by_matrix(part):
            part = part.reshape(own_rows, head_pairs, 3, 128)
            return part.transpose(2, 0, 1, 3).reshape(3, own_rows, half_width)

        qkv_sum = in_order(
            by_matrix(dpack[:, :columns]), by_matrix(dpack[:, columns : 2 * columns]), y, 2
        )
        attention_sum = jnp.concatenate([qkv_sum, dout_sum[None]], axis=0)
        vector_sum = dpack[:, 2 * columns :][:, : 4 + NEXP].T

        attention_m, attention_s, attention_u = moments(
            attention_master, attention_first, attention_second, attention_sum
        )
        vector_m, vector_s, vector_u = moments(
            vector_master, vector_first, vector_second, vector_sum
        )
        expert_m, expert_s, expert_u = moments(
            expert_master, expert_first, expert_second, expert_sum
        )

        def squares(attention_x, vector_x, expert_x):
            vector_parts = jnp.sum(vector_x * vector_x, axis=1)
            expert_parts = lax.dynamic_update_slice_in_dim(
                jnp.zeros((NFFN * 3,), f32),
                jnp.sum(expert_x * expert_x, axis=(2, 3)).reshape(-1),
                s * local_experts * 3,
                0,
            )
            return jnp.concatenate(
                [
                    jnp.sum(attention_x * attention_x, axis=(1, 2)),
                    vector_parts[0:2],
                    jnp.sum(vector_parts[2:4])[None],
                    jnp.sum(vector_parts[4:])[None],
                    expert_parts,
                ]
            )

        count = 8 + 3 * NFFN
        small = jnp.concatenate(
            [
                squares(attention_master, vector_master, expert_master),
                squares(attention_u, vector_u, expert_u),
                dmixing.reshape(-1),
            ]
        )
        used = small.shape[0]
        small = jnp.pad(small, (0, -used % 128)).reshape(-1, 128)
        small = sum_everywhere(small, sizes).reshape(-1)
        summed_squares = small[: 2 * count].reshape(2, count)
        mixing_grad = small[2 * count : used].reshape(NEXP, NEXP)
        mixing_m, mixing_s, mixing_u = moments(
            mixing_master, mixing_first, mixing_second, mixing_grad
        )
        mixing_squares = jnp.stack(
            [jnp.sum(mixing_master * mixing_master), jnp.sum(mixing_u * mixing_u)]
        )
        tensor_norms = jnp.sqrt(jnp.concatenate([summed_squares, mixing_squares[:, None]], axis=1))
        ratios = learn_rate * (tensor_norms[0] / (tensor_norms[1] + norm_eps))
        vector_ratio = jnp.concatenate(
            [
                ratios[4:6],
                jnp.broadcast_to(ratios[6:7], (2,)),
                jnp.broadcast_to(ratios[7:8], (NEXP,)),
            ]
        )[:, None]
        expert_ratio = lax.dynamic_slice_in_dim(
            ratios[8:count].reshape(NFFN, 3), s * local_experts, local_experts, 0
        )[:, :, None, None]
        return (
            block_output[None],
            input_gradient[None],
            attention_master - ratios[0:4][:, None, None] * attention_u,
            vector_master - vector_ratio * vector_u,
            expert_master - expert_ratio * expert_u,
            mixing_master - ratios[count] * mixing_u,
            attention_m,
            vector_m,
            expert_m,
            mixing_m,
            attention_s,
            vector_s,
            expert_s,
            mixing_s,
            tensor_norms,
        )

    return shards


def solution(mesh):
    n_dp, n_seq, n_shard = (mesh.shape[name] for name in ("dp", "seq", "shard"))
    finer = jax.sharding.Mesh(
        mesh.devices.reshape(n_dp // 2, 2, n_seq, n_shard // 2, 2), DP + ("seq",) + SHARD
    )
    tokens_spec = P(DP + SHARD, "seq", None)
    attention_spec = P(None, DP + ("seq",) + SHARD, None)
    vector_spec = P(None, DP + ("seq",) + SHARD)
    expert_spec = P(SHARD, None, DP + ("seq",), None)
    weights = (attention_spec, vector_spec, expert_spec, P())
    return jax.shard_map(
        make_shards(dict(finer.shape)),
        mesh=finer,
        in_specs=(tokens_spec,) * 5 + weights * 3,
        out_specs=(tokens_spec,) * 2 + weights * 3 + (P(),),
        check_vma=False,
    )
```

```python
import jax
import jax.numpy as jnp
import numpy as np
from jax import lax
from jax.experimental import pallas as pl
from jax.experimental.layout import Layout, with_layout_constraint
from jax.experimental.pallas import tpu as pltpu
from jax.sharding import PartitionSpec as P

HEADS = 12
HDIM = 64
NFFN = 8
TOP = 2
STEP = 4
NEXP = 12

beta_one = 0.9
beta_two = 0.999
adam_eps = 1e-06
weight_decay = 0.01
learn_rate = 0.25
norm_eps = 1e-06
rope_base = 10000.0

bf16 = jnp.bfloat16
f32 = jnp.float32


def exact_dot(left, right):
    return jnp.dot(left, right, precision=lax.Precision.HIGHEST, preferred_element_type=f32)


def dot_nn(left, right):
    return lax.dot_general(left, right, (((1,), (0,)), ((), ())), preferred_element_type=f32)


def dot_nt(left, right):
    return lax.dot_general(left, right, (((1,), (1,)), ((), ())), preferred_element_type=f32)


def dot_tn(left, right):
    return lax.dot_general(left, right, (((0,), (0,)), ((), ())), preferred_element_type=f32)


def rotary_tables(length):
    freqs = np.float32(rope_base) ** (-np.arange(0, HDIM, 2).astype(np.float32) / np.float32(HDIM))
    angles = np.arange(length).astype(np.float32)[:, None] * freqs[None, :]
    cosine = np.cos(angles.astype(np.float64)).astype(np.float32)
    sine = np.sin(angles.astype(np.float64)).astype(np.float32)
    return (
        jnp.asarray(np.concatenate([cosine] * 4, axis=-1)),
        jnp.asarray(np.concatenate([-sine, sine, -sine, sine], axis=-1)),
    )


def softmax_rows(logits):
    row_top = jnp.max(logits, axis=-1, keepdims=True)
    expd_values = jnp.exp(logits - row_top)
    return expd_values / jnp.sum(expd_values, axis=-1, keepdims=True)


def moments(weight, first, second, grad):
    first_new = beta_one * first + (1.0 - beta_one) * grad
    second_new = beta_two * second + (1.0 - beta_two) * grad * grad
    step_value = (
        first_new
        / (1.0 - beta_one**STEP)
        / (jnp.sqrt(second_new / (1.0 - beta_two**STEP)) + adam_eps)
        + weight_decay * weight
    )
    return (first_new, second_new, step_value)


DP = ("dp_far", "dp_near")
SHARD = ("x", "core")


def after(value, *others):
    return lax.optimization_barrier((value,) + others)[0]


def swap(value, axis_name):
    return lax.ppermute(value, axis_name, [(0, 1), (1, 0)])


def swap_seq(value):
    return swap(value, "seq")


def in_order(own, other, which, axis):
    low = jnp.where(which == 0, own, other)
    high = jnp.where(which == 0, other, own)
    return jnp.concatenate([low, high], axis=axis)


def gather_steps(value, axis_name, place, count):
    out = jnp.zeros((count,) + value.shape, value.dtype)
    out = lax.dynamic_update_index_in_dim(out, value, place, 0)
    for step in range(1, count):
        got = lax.ppermute(value, axis_name, [(i, (i + step) % count) for i in range(count)])
        out = lax.dynamic_update_index_in_dim(out, got, (place - step) % count, 0)
    return out


def scatter_steps(value, axis_name, place, count, wait_for=()):
    total = lax.dynamic_index_in_dim(value, place, 0, keepdims=False).astype(f32)
    got = []
    for step in range(1, count):
        block = lax.dynamic_index_in_dim(value, (place + step) % count, 0, keepdims=False)
        got.append(lax.ppermute(block, axis_name, [(i, (i + step) % count) for i in range(count)]))
    for part in after(got, wait_for):
        total = total + part.astype(f32)
    return total


def keep_and_send(value, place, axis):
    return (
        lax.dynamic_index_in_dim(value, place, axis, keepdims=False),
        lax.dynamic_index_in_dim(value, 1 - place, axis, keepdims=False),
    )


def sum_everywhere(value, sizes):
    for axis_names in (("core",), ("seq", "x"), DP):
        count = 1
        for name in axis_names:
            count *= sizes[name]
        rounds = [[1 << bit] for bit in range(count.bit_length() - 1)]
        if count <= 4:
            rounds = [range(1, count)]
        for steps in rounds:
            got = [
                lax.ppermute(value, axis_names, [(i, i ^ step) for i in range(count)])
                for step in steps
            ]
            if len(got) == 3:
                value = (value + got[0]) + (got[1] + got[2])
            else:
                value = value + got[0]
    return value


QUERY_ROWS = 256
FF_COLUMNS = 512

def turn(value):
    lane = lax.broadcasted_iota(jnp.int32, value.shape, 1) % HDIM
    return jnp.where(lane < HDIM // 2, pltpu.roll(value, 96, 1), pltpu.roll(value, 32, 1))

def attention_forward_kernel(x_ref, gain_ref, wq_ref, wk_ref, wv_ref, cos_ref, sin_ref, h_ref, q_ref, k_ref, v_ref, o_ref, lse_ref):
    length = x_ref.shape[0]

    @pl.when(pl.program_id(0) == 0)
    def _():
        for start in range(0, length, QUERY_ROWS):
            rows = pl.ds(start, QUERY_ROWS)
            x = x_ref[rows, :].astype(f32)
            rho = lax.rsqrt(jnp.mean(x * x, axis=-1, keepdims=True) + norm_eps)
            h_ref[rows, :] = (x * rho * gain_ref[...]).astype(bf16)

    for start in range(0, length, QUERY_ROWS):
        rows = pl.ds(start, QUERY_ROWS)
        h = h_ref[rows, :]
        cos, sin = cos_ref[rows, :], sin_ref[rows, :]
        q = dot_nn(h, wq_ref[...])
        k = dot_nn(h, wk_ref[...])
        q_ref[rows, :] = (q * cos + turn(q) * sin).astype(bf16)
        k_ref[rows, :] = (k * cos + turn(k) * sin).astype(bf16)
        v_ref[rows, :] = dot_nn(h, wv_ref[...]).astype(bf16)

    ahead = lax.broadcasted_iota(jnp.int32, (QUERY_ROWS, QUERY_ROWS), 1) > lax.broadcasted_iota(jnp.int32, (QUERY_ROWS, QUERY_ROWS), 0)
    for start in range(0, length, QUERY_ROWS):
        end = start + QUERY_ROWS
        outs = []
        for head in range(2):
            lanes = slice(head * HDIM, (head + 1) * HDIM)
            q = q_ref[start:end, lanes]
            s = dot_nt(q, k_ref[:end, lanes]) * (HDIM**-0.5)
            last = jnp.where(ahead, -1e30, s[:, start:])
            s = jnp.concatenate([s[:, :start], last], axis=1) if start else last
            top = jnp.max(s, axis=-1, keepdims=True)
            p = jnp.exp(s - top)
            total = jnp.sum(p, axis=-1, keepdims=True)
            p = (p * (1.0 / total)).astype(bf16)
            outs.append(dot_nn(p, v_ref[:end, lanes]))
            lse = jnp.broadcast_to(top + jnp.log(total), (QUERY_ROWS, 128))
            lse_ref[0, head : head + 1, start:end] = lse.T[0:1, :]
        o_ref[start:end, :] = jnp.concatenate(outs, axis=1).astype(bf16)

def attention_forward(x, gain, weight, cos, sin):
    length, width = x.shape
    half = weight.shape[1] // 3
    pairs = half // 128
    full = lambda shape: pl.BlockSpec(shape, lambda p: (0,) * len(shape))
    col = lambda base: pl.BlockSpec((width, 128), lambda p, base=base: (0, base + p))
    out_col = pl.BlockSpec((length, 128), lambda p: (0, p))
    return pl.pallas_call(
        attention_forward_kernel,
        grid=(pairs,),
        in_specs=[full((length, width)), full((1, width)), col(0), col(pairs), col(2 * pairs), full((length, 128)), full((length, 128))],
        out_specs=[full((length, width)), out_col, out_col, out_col, out_col, pl.BlockSpec((1, 2, length), lambda p: (p, 0, 0))],
        out_shape=[jax.ShapeDtypeStruct((length, width), bf16)] + [jax.ShapeDtypeStruct((length, half), bf16)] * 4 + [jax.ShapeDtypeStruct((pairs, 2, length), f32)],
        compiler_params=pltpu.CompilerParams(vmem_limit_bytes=40 * 2**20),
        cost_estimate=pl.CostEstimate(flops=6 * length * width * half + 4 * length * length * half, bytes_accessed=8 * length * width, transcendentals=length * length * half // HDIM),
    )(x, gain, weight, weight, weight, cos, sin)

def attention_backward_kernel(h_ref, x_ref, vector_ref, q_ref, k_ref, v_ref, do_ref, lse_ref, wq_ref, wk_ref, wv_ref, cos_ref, sin_ref, dw_ref, dh_ref, dq_scr, dk_scr, dv_scr):
    length = h_ref.shape[0]
    step = pl.program_id(0)
    behind = lax.broadcasted_iota(jnp.int32, (QUERY_ROWS, QUERY_ROWS), 0) > lax.broadcasted_iota(jnp.int32, (QUERY_ROWS, QUERY_ROWS), 1)
    dk_scr[...] = jnp.zeros_like(dk_scr)
    dv_scr[...] = jnp.zeros_like(dv_scr)
    for start in range(0, length, QUERY_ROWS):
        end = start + QUERY_ROWS
        for head in range(2):
            lanes = slice(head * HDIM, (head + 1) * HDIM)
            q, do = q_ref[start:end, lanes], do_ref[start:end, lanes]
            k, v = k_ref[:end, lanes], v_ref[:end, lanes]
            s = dot_nt(k, q) * (HDIM**-0.5) - lse_ref[0, head : head + 1, start:end]
            last = jnp.where(behind, -1e30, s[start:])
            s = jnp.concatenate([s[:start], last], axis=0) if start else last
            p = jnp.exp(s)
            dp = dot_nt(v, do)
            delta = jnp.sum(p * dp, axis=0, keepdims=True)
            ds = (p * (dp - delta)).astype(bf16)
            dq_scr[start:end, lanes] = dot_tn(ds, k) * (HDIM**-0.5)
            dk_scr[:end, lanes] += dot_nn(ds, q)
            dv_scr[:end, lanes] += dot_nn(p.astype(bf16), do)
    cos, sin = cos_ref[...], sin_ref[...]

    dq = dq_scr[...].astype(bf16).astype(f32)
    dk = (dk_scr[...] * (HDIM**-0.5)).astype(bf16).astype(f32)
    dqp = (dq * cos + turn(dq * sin)).astype(bf16)
    dkp = (dk * cos + turn(dk * sin)).astype(bf16)
    dvb = dv_scr[...].astype(bf16)
    d = jnp.concatenate([dqp, dkp, dvb], axis=1)
    w = jnp.concatenate([wq_ref[...], wk_ref[...], wv_ref[...]], axis=1)
    columns = d.shape[1]
    place = pl.ds(pl.multiple_of(step * columns, 128), columns)
    dw_ref[:, place] = dot_tn(h_ref[...], d).astype(bf16)
    dh = dot_nt(d, w)

    @pl.when(step == 0)
    def _():
        dh_ref[...] = dh

    @pl.when(step > 0)
    def _():
        dh_ref[...] += dh

    @pl.when(step == pl.num_programs(0) - 1)
    def _():
        dgain = jnp.zeros((1, x_ref.shape[1]), f32)
        for start in range(0, length, QUERY_ROWS):
            rows = pl.ds(start, QUERY_ROWS)
            x = x_ref[rows, :].astype(f32)
            rho = lax.rsqrt(jnp.mean(x * x, axis=-1, keepdims=True) + norm_eps)
            dgain += jnp.sum(dh_ref[rows, :] * (x * rho), axis=0, keepdims=True)
        turned = jnp.broadcast_to(dgain, (128, x_ref.shape[1])).T
        lane = lax.broadcasted_iota(jnp.int32, turned.shape, 1)
        vectors = jnp.where(lane == 0, turned, vector_ref[...])
        dw_ref[:, dw_ref.shape[1] - 128 :] = vectors.astype(bf16)

def attention_backward(h, x, vectors, q, k, v, do, lse, weight, cos, sin):
    length, width = h.shape
    half = weight.shape[1] // 3
    pairs = half // 128
    full = lambda shape: pl.BlockSpec(shape, lambda p: (0,) * len(shape))
    col = lambda base: pl.BlockSpec((width, 128), lambda p, base=base: (0, base + p))
    out_col = pl.BlockSpec((length, 128), lambda p: (0, p))
    return pl.pallas_call(
        attention_backward_kernel,
        grid=(pairs,),
        in_specs=[full((length, width)), full((length, width)), full((width, 128)), out_col, out_col, out_col, out_col, pl.BlockSpec((1, 2, length), lambda p: (p, 0, 0)), col(0), col(pairs), col(2 * pairs), full((length, 128)), full((length, 128))],
        out_specs=[full((width, 3 * half + 128)), full((length, width))],
        out_shape=[jax.ShapeDtypeStruct((width, 3 * half + 128), bf16), jax.ShapeDtypeStruct((length, width), f32)],
        scratch_shapes=[pltpu.VMEM((length, 128), f32)] * 3,
        compiler_params=pltpu.CompilerParams(vmem_limit_bytes=48 * 2**20),
        cost_estimate=pl.CostEstimate(flops=12 * length * width * half + 10 * length * length * half, bytes_accessed=12 * length * width, transcendentals=length * length * half // HDIM),
    )(h, x, vectors, q, k, v, do, lse, weight, weight, weight, cos, sin)


def gate_columns(value, which):
    high = lax.reduce_precision(value, 8, 7)
    middle = lax.reduce_precision(value - high, 8, 7)
    low = lax.reduce_precision(value - high - middle, 8, 7)
    lane = lax.broadcasted_iota(jnp.int32, (value.shape[0], 128), 1)
    columns = jnp.where(lane == 3, 1.0 * which, 0.0)
    for part, place in ((high, 0), (middle, 1), (low, 2)):
        columns = jnp.where(lane == place + 4 * which, part, columns)
    return columns.astype(bf16)


def expert_kernel(
    flipped_ref,
    taken_ref,
    dout_ref,
    same_ref,
    other_ref,
    f_ref,
    dtaken_ref,
    right_ref,
    dresult_ref,
    weight_ref,
    f_acc,
    d_acc,
):
    step, last = pl.program_id(0), pl.num_programs(0) - 1
    width = dout_ref.shape[1]

    @pl.when(step == 0)
    def _():
        lanes = taken_ref[:, width:].astype(f32)
        lane = lax.broadcasted_iota(jnp.int32, lanes.shape, 1)
        gate = jnp.sum(jnp.where(lane == 3, 0.0, lanes), axis=1, keepdims=True)
        dresult_ref[...] = (gate * dout_ref[...].astype(f32)).astype(bf16)

    eighth = width // 8
    shift = flipped_ref[0] * eighth
    for matrix in range(3):
        for pair in range(4):
            rows = slice(pair * eighth, (pair + 1) * eighth)
            base = 2 * pair * eighth
            place = pl.ds(pl.multiple_of(base + shift, 32), eighth)
            weight_ref[matrix, place, :] = same_ref[matrix, rows, :]
            place = pl.ds(pl.multiple_of(base + eighth - shift, 32), eighth)
            weight_ref[matrix, place, :] = other_ref[matrix, rows, :]
    taken = taken_ref[:, :width]
    a = dot_nn(taken, weight_ref[0])
    b = dot_nn(taken, weight_ref[1])
    sig = jax.nn.sigmoid(a)
    act = a * sig
    hidden = (act * b).astype(bf16)
    right_ref[2] = hidden
    dhidden = dot_nn(dresult_ref[...], weight_ref[2])
    dgate = (dhidden * b * (sig * (1.0 + a - act))).astype(bf16)
    dup = (dhidden * act).astype(bf16)
    right_ref[0] = dgate
    right_ref[1] = dup
    f = dot_nt(hidden, weight_ref[2])
    d = dot_nt(dgate, weight_ref[0]) + dot_nt(dup, weight_ref[1])

    @pl.when(step == 0)
    def _():
        f_acc[...] = f
        d_acc[...] = d

    @pl.when(step > 0)
    def _():
        f_acc[...] += f
        d_acc[...] += d

    @pl.when(step == last)
    def _():
        f = f_acc[...].astype(bf16)
        f_ref[...] = f
        dtaken_ref[:, :width] = d_acc[...].astype(bf16)
        dpicked = jnp.sum(dout_ref[...].astype(f32) * f.astype(f32), axis=1, keepdims=True)
        high = dpicked.astype(bf16).astype(f32)
        middle = (dpicked - high).astype(bf16).astype(f32)
        low = (dpicked - high - middle).astype(bf16).astype(f32)
        lanes = taken_ref[:, width:].astype(f32)
        lane = lax.broadcasted_iota(jnp.int32, lanes.shape, 1)
        second = jnp.sum(jnp.where(lane == 3, lanes, 0.0), axis=1, keepdims=True)
        mine = jnp.where(lane < 3, 1.0 - second, jnp.where((lane > 3) & (lane < 7), second, 0.0))
        part = jnp.where(lane % 4 == 0, high, jnp.where(lane % 4 == 1, middle, low))
        dtaken_ref[:, width:] = (mine * part).astype(bf16)


def expert_compute(flipped, taken, dout, same, other):
    rows, width = dout.shape
    hidden = same.shape[2]
    half = pl.BlockSpec((3, width // 2, FF_COLUMNS), lambda i: (0, 0, i))
    whole = lambda columns: pl.BlockSpec((rows, columns), lambda i: (0, 0))
    shape = lambda columns: jax.ShapeDtypeStruct((rows, columns), bf16)
    return pl.pallas_call(
        expert_kernel,
        grid=(hidden // FF_COLUMNS,),
        in_specs=[
            pl.BlockSpec(memory_space=pltpu.SMEM),
            whole(width + 128),
            whole(width),
            half,
            half,
        ],
        out_specs=[
            whole(width),
            whole(width + 128),
            pl.BlockSpec((3, rows, FF_COLUMNS), lambda i: (0, 0, i)),
            whole(width),
        ],
        out_shape=[
            shape(width),
            shape(width + 128),
            jax.ShapeDtypeStruct((3, rows, hidden), bf16),
            shape(width),
        ],
        scratch_shapes=[pltpu.VMEM((3, width, FF_COLUMNS), bf16)] + [pltpu.VMEM((rows, width), f32)] * 2,
        compiler_params=pltpu.CompilerParams(vmem_limit_bytes=48 * 2**20),
        cost_estimate=pl.CostEstimate(
            flops=14 * rows * width * hidden,
            bytes_accessed=6 * width * hidden + 6 * rows * hidden,
            transcendentals=rows * hidden,
        ),
    )(flipped, taken, dout, same, other)


def gradient_kernel(taken_ref, dresult_ref, right_ref, out_ref, turned):
    step, first_down = pl.program_id(0), 2 * pl.num_programs(0) // 3
    width = dresult_ref.shape[1]

    @pl.when(step == 0)
    def _():
        turned[...] = taken_ref[:, :width].T

    @pl.when(step == first_down)
    def _():
        turned[...] = dresult_ref[...].T

    out_ref[...] = dot_nn(turned[...], right_ref[0]).astype(bf16)


def weight_gradients(taken, dresult, right):
    rows, width = dresult.shape
    columns = right.shape[2]
    tile = min(columns, 2 * FF_COLUMNS)
    steps = columns // tile
    return pl.pallas_call(
        gradient_kernel,
        grid=(3 * steps,),
        in_specs=[
            pl.BlockSpec((rows, taken.shape[1]), lambda i: (0, 0)),
            pl.BlockSpec((rows, width), lambda i: (0, 0)),
            pl.BlockSpec((1, rows, tile), lambda i: (i // steps, 0, i % steps)),
        ],
        out_specs=pl.BlockSpec((width, tile), lambda i: (0, i)),
        out_shape=jax.ShapeDtypeStruct((width, 3 * columns), bf16),
        scratch_shapes=[pltpu.VMEM((width, rows), bf16)],
        compiler_params=pltpu.CompilerParams(vmem_limit_bytes=58 * 2**20),
        cost_estimate=pl.CostEstimate(
            flops=6 * rows * width * columns,
            bytes_accessed=6 * (rows + width) * columns,
            transcendentals=0,
        ),
    )(taken, dresult, right)


def make_shards(sizes):
    n_seq, n_x = sizes["seq"], sizes["x"]
    n_dp = sizes["dp_far"] * sizes["dp_near"]

    def shards(
        tokens,
        cotangent,
        previous_logits,
        routes,
        priority,
        attention_master,
        vector_master,
        expert_master,
        mixing_master,
        attention_first,
        vector_first,
        expert_first,
        mixing_first,
        attention_second,
        vector_second,
        expert_second,
        mixing_second,
    ):
        z, y, s = lax.axis_index(DP), lax.axis_index("seq"), lax.axis_index(SHARD)
        far, near = lax.axis_index("dp_far"), lax.axis_index("dp_near")
        x_place, core = lax.axis_index("x"), lax.axis_index("core")
        row_count, model_width = tokens.shape[1], tokens.shape[2]
        half_width = model_width // 2
        local_experts = expert_master.shape[0]
        spread = local_experts == 2 and n_x == 2 and sizes["dp_far"] == 2
        ep_axes = ("dp_near", "seq", "x") if spread else SHARD
        ep_place = lax.axis_index(ep_axes)
        own_rows = attention_master.shape[1]

        def cross(same_y, other_y):
            got = lax.ppermute(same_y, ("dp_near", "core"), [(1, 2), (2, 1)])
            moves = [
                (4 * n + 2 * q + c, 4 * c + 2 * (1 - q) + n)
                for n in range(2)
                for q in range(2)
                for c in range(2)
            ]
            return (
                jnp.where(near == core, same_y, got),
                lax.ppermute(other_y, ("dp_near", "seq", "core"), moves),
            )

        attention_low = attention_master.astype(bf16)
        vector_low = vector_master.astype(bf16).T
        vector_pad = 128 - vector_low.shape[1]

        def weight_pack(which):
            columns = lax.dynamic_slice_in_dim(attention_low[:3], which * half_width, half_width, 2)
            return jnp.concatenate(
                [columns[0], columns[1], columns[2], attention_low[3], jnp.pad(vector_low, ((0, 0), (0, vector_pad)))],
                axis=1,
            )

        packed = in_order(weight_pack(y)[None], swap_seq(weight_pack(1 - y))[None], y, 0)

        packed_z = gather_steps(packed, DP, z, n_dp)
        packed_x = gather_steps(packed_z, "x", x_place, n_x)
        expert_low = after(expert_master, packed).astype(bf16)
        if spread:
            same_y, other_y = cross(*keep_and_send(expert_low, y, 0))
            expert_same = lax.all_gather(
                after(same_y, packed_z), ("dp_far", "core"), axis=1, tiled=True
            )
            expert_other = lax.all_gather(
                after(other_y, packed_z), ("dp_far", "core"), axis=1, tiled=True
            )
            flipped = y
        else:
            expert_use = lax.all_gather(expert_low[0], DP + ("seq",), axis=1, tiled=True)
            expert_use = expert_use.reshape(3, 4, 2, model_width // 8, -1)
            expert_same = expert_use[:, :, 0].reshape(3, model_width // 2, -1)
            expert_other = expert_use[:, :, 1].reshape(3, model_width // 2, -1)
            flipped = jnp.zeros_like(y)

        packed = packed_x
        packed = in_order(packed[None], swap(packed, "core")[None], core, 0)
        packed = packed.transpose(2, 3, 1, 0, 4, 5).reshape(model_width, -1)
        qkv_weight = packed[:, : 3 * half_width]
        out_weight = packed[:, 3 * half_width : 3 * half_width + model_width]
        vector_all = packed[:, 3 * half_width + model_width :][:, : 4 + NEXP].T

        route_rows = routes[0]
        order = priority[0, 0]
        capacity = 9 * row_count * TOP // (8 * NEXP)
        expert_ids = jnp.arange(NEXP)[None, :]
        hit_each = [route_rows[:, j : j + 1] == expert_ids for j in range(TOP)]
        hits = (hit_each[0] | hit_each[1]).astype(bf16)
        before = (order[None, :] < order[:, None]).astype(bf16)
        counts = dot_nn(before, hits)
        kept, dispatch = [], []
        block_ids = jnp.arange(NFFN * capacity)[None, :]
        for j in range(TOP):
            slot = jnp.sum(jnp.where(hit_each[j], counts, 0.0), axis=1, keepdims=True).astype(
                jnp.int32
            )
            route = route_rows[:, j : j + 1]
            keep = (route < NFFN) & (slot < capacity)
            block = ((route // 2) % 2) * 4 + (route % 2) * 2 + route // 4 if spread else route
            block = block ^ ep_place
            kept.append(keep)
            dispatch.append(
                ((block_ids == block * capacity + slot) & keep).astype(bf16)
            )
        dispatch_both = dispatch[0] + dispatch[1]

        tokens_all = in_order(tokens[0], swap_seq(tokens[0]), y, 0)
        gain_one = vector_all[0].astype(f32)[None, :]
        gain_two = vector_all[1].astype(f32)[None, :]
        cosine, sine = rotary_tables(tokens_all.shape[0])
        normed, query, key, value, mixed, log_sums = attention_forward(
            tokens_all, gain_one, qkv_weight, cosine, sine
        )

        upstream = cotangent[0].astype(f32)
        def exchange(rows):
            blocks = rows.reshape(NFFN, capacity, rows.shape[1])
            return [blocks[0]] + [
                lax.ppermute(blocks[k], ep_axes, [(i, i ^ k) for i in range(NFFN)])
                for k in range(1, NFFN)
            ]

        def exchanged(rows):
            return jnp.concatenate(exchange(rows), axis=0)

        dout_rows = dot_tn(dispatch_both, cotangent[0]).astype(bf16)
        dout_rows = exchange(after(dout_rows, tokens_all))
        mixed, dout_rows = lax.optimization_barrier((mixed, dout_rows))

        mixed_keep = lax.dynamic_slice_in_dim(mixed, y * row_count, row_count, 0)
        mixed_send = lax.dynamic_slice_in_dim(mixed, (1 - y) * row_count, row_count, 0)
        mixed_tokens = in_order(mixed_keep, swap_seq(mixed_send), y, 1)

        inputs = tokens[0].astype(f32)
        resid = inputs + dot_nn(mixed_tokens, out_weight)
        rho_two = lax.rsqrt(jnp.mean(resid * resid, axis=-1, keepdims=True) + norm_eps)
        normed_two = resid * rho_two * gain_two
        expert_in = normed_two.astype(bf16)
        router = vector_all[4:]
        previous = previous_logits[0]
        logits = dot_nt(expert_in, router) + exact_dot(previous, mixing_master)
        gates = softmax_rows(logits)
        picked = [
            jnp.sum(jnp.where(hit_each[j], gates, 0.0), axis=1, keepdims=True) for j in range(TOP)
        ]

        consts = vector_all[2:4].astype(f32)
        dlocal = [
            jnp.sum(upstream * normed_two, axis=-1, keepdims=True),
            jnp.sum(upstream * consts[0:1], axis=-1, keepdims=True),
            jnp.sum(upstream * consts[1:2], axis=-1, keepdims=True),
        ]

        taken = dot_tn(
            jnp.concatenate(dispatch, axis=0),
            jnp.concatenate(
                [
                    jnp.concatenate([expert_in, gate_columns(picked[j], j)], axis=1)
                    for j in range(TOP)
                ],
                axis=0,
            ),
        ).astype(bf16)
        taken = exchanged(taken)
        dout_rows = jnp.concatenate(dout_rows, axis=0)
        result, dtaken, right, dresult = expert_compute(
            flipped[None].astype(jnp.int32), taken, dout_rows, expert_same, expert_other
        )
        dtaken = exchange(dtaken)
        dtaken = jnp.concatenate(dtaken, axis=0)

        def sum_rows(grad):
            axes = ("dp_far", "core") if spread else DP + ("seq",)
            return lax.psum_scatter(grad, axes, scatter_dimension=0, tiled=True)

        def to_owners(same_y, other_y):
            if not spread:
                return same_y[None]
            same_y, other_y = cross(same_y, other_y)
            return in_order(same_y[None], other_y[None], y, 0)

        hidden_width = right.shape[2]
        dexpert = weight_gradients(taken, dresult, right)
        result = exchange(after(result, dtaken))
        dexpert = sum_rows(dexpert)
        if spread:
            row_parts = keep_and_send(dexpert.reshape(2, -1, dexpert.shape[1]), y, 0)
        else:
            row_parts = (dexpert, dexpert)


        dgates = jnp.zeros_like(gates)
        returned = dot_nn(dispatch_both, dtaken)
        dnormed_two = returned[:, :model_width]
        value_weight = [0.0, 0.0, 0.0]
        for j in range(TOP):
            route = route_rows[:, j : j + 1]
            local = [jnp.where(route == NFFN + 1 + i, 1.0, 0.0) for i in range(3)]
            parts = returned[:, model_width + 4 * j : model_width + 4 * j + 3]
            dpicked = jnp.sum(parts, axis=1, keepdims=True)
            for i in range(3):
                dpicked = dpicked + jnp.where(route == NFFN + 1 + i, dlocal[i], 0.0)
                value_weight[i] = value_weight[i] + local[i] * picked[j]
            dgates = dgates + jnp.where(hit_each[j], dpicked, 0.0)
        dnormed_two = dnormed_two + value_weight[0] * upstream
        dconst_one = jnp.sum(value_weight[1] * upstream, axis=0, keepdims=True)
        dconst_two = jnp.sum(value_weight[2] * upstream, axis=0, keepdims=True)
        dlogits = gates * (dgates - jnp.sum(gates * dgates, axis=-1, keepdims=True))
        dnormed_two = dnormed_two + exact_dot(dlogits, router.astype(f32))
        drouter = exact_dot(dlogits.T, expert_in.astype(f32))
        dmixing = exact_dot(previous.T, dlogits)
        scaled_two = dnormed_two * gain_two
        dresid = upstream + (
            rho_two * scaled_two
            - resid * (rho_two * rho_two * rho_two) * jnp.mean(resid * scaled_two, -1, keepdims=True)
        )
        dgain_two = jnp.sum(dnormed_two * resid * rho_two, axis=0, keepdims=True)
        dbranch_low = dresid.astype(bf16)
        dweight_out = dot_tn(mixed_tokens, dbranch_low)

        group, place = n_seq * n_x, y * n_x + x_place

        def core_sum(grad):
            grad = grad.astype(bf16).reshape(n_dp, n_seq, n_x, 2, own_rows, -1)
            keep, send = keep_and_send(grad.transpose(3, 1, 2, 0, 4, 5), core, 0)
            return (keep.astype(f32) + swap(send, "core").astype(f32)).astype(bf16)

        def plane_sum(grad):
            grad = grad.reshape((group,) + grad.shape[2:])
            totals = [lax.dynamic_index_in_dim(grad, place, 0, keepdims=False).astype(f32), 0.0]
            for step in range(1, group):
                block = lax.dynamic_index_in_dim(grad, place ^ step, 0, keepdims=False)
                got = lax.ppermute(block, ("seq", "x"), [(i, i ^ step) for i in range(group)])
                totals[step // n_x] = totals[step // n_x] + got.astype(f32)
            return totals

        def dp_sum(grad, wait_for):
            return scatter_steps(grad.astype(bf16), DP, z, n_dp, wait_for)

        dmixed = dot_nt(dbranch_low, out_weight).astype(bf16)
        dmixed_keep = lax.dynamic_slice_in_dim(dmixed, y * half_width, half_width, 1)
        dmixed_send = lax.dynamic_slice_in_dim(dmixed, (1 - y) * half_width, half_width, 1)
        dmixed_heads = in_order(dmixed_keep, swap_seq(dmixed_send), y, 0)
        dout_part = core_sum(dweight_out)
        vectors = jnp.concatenate(
            [jnp.zeros_like(dgain_two), dgain_two, dconst_one, dconst_two, drouter], axis=0
        )
        vectors = jnp.pad(vectors.T, ((0, 0), (0, vector_pad)))
        dpack, dnormed_all = attention_backward(
            normed, tokens_all, vectors, query, key, value, dmixed_heads, log_sums, qkv_weight, cosine, sine
        )
        dpack, result = after((dpack, result), dnormed_all)
        dpack = after(dpack, result)
        this_y, other_y = plane_sum(jnp.concatenate([core_sum(dpack), dout_part], axis=-1))
        columns = 3 * half_width
        dpack = dp_sum(
            (
                jnp.concatenate(
                    [
                        this_y[..., :columns],
                        other_y[..., :columns],
                        this_y[..., columns:] + other_y[..., columns:],
                    ],
                    axis=-1,
                ).astype(bf16)
            ),
            row_parts,
        )
        dnormed_keep = lax.dynamic_slice_in_dim(dnormed_all, y * row_count, row_count, 0)
        dnormed_send = lax.dynamic_slice_in_dim(
            dnormed_all, (1 - y) * row_count, row_count, 0
        )
        dnormed = dnormed_keep + swap_seq(dnormed_send.astype(bf16)).astype(f32)
        rho_one = lax.rsqrt(jnp.mean(inputs * inputs, axis=-1, keepdims=True) + norm_eps)
        scaled_one = dnormed * gain_one
        input_gradient = dresid + (
            rho_one * scaled_one
            - inputs * (rho_one * rho_one * rho_one) * jnp.mean(inputs * scaled_one, -1, keepdims=True)
        )
        dpack = after(dpack, dexpert)
        result = jnp.concatenate(result, axis=0)
        mixture = (
            picked[0] * dot_nn(dispatch[0], result)
            + picked[1] * dot_nn(dispatch[1], result)
            + value_weight[0] * normed_two
            + value_weight[1] * consts[0:1]
            + value_weight[2] * consts[1:2]
        )
        block_output = (resid + mixture).astype(bf16)
        dpack = with_layout_constraint(dpack, Layout((0, 1)))
        head_pairs = half_width // 128

        def by_matrix(part):
            return jnp.stack(
                [
                    jnp.concatenate(
                        [
                            part[:, 384 * pair + 128 * which : 384 * pair + 128 * which + 128]
                            for pair in range(head_pairs)
                        ],
                        axis=1,
                    )
                    for which in range(3)
                ]
            )

        qkv_sum = in_order(
            by_matrix(dpack[:, :columns]), by_matrix(dpack[:, columns : 2 * columns]), y, 2
        )
        vector_sum = dpack[:, 2 * columns :][:, : 4 + NEXP].T
        dout_sum = dpack[:, 2 * columns + 128 :]
        attention_sum = jnp.concatenate([qkv_sum, dout_sum[None]], axis=0)

        attention_m, attention_s, attention_u = moments(
            attention_master, attention_first, attention_second, attention_sum
        )
        vector_m, vector_s, vector_u = moments(
            vector_master, vector_first, vector_second, vector_sum
        )
        dexpert = to_owners(*row_parts)
        expert_sum = jnp.stack(jnp.split(dexpert, 3, axis=2), axis=1).astype(f32)
        expert_m, expert_s, expert_u = moments(
            expert_master, expert_first, expert_second, expert_sum
        )

        expert_u = lax.optimization_barrier(expert_u)

        def squares(attention_x, vector_x, expert_x):
            vector_parts = jnp.sum(vector_x * vector_x, axis=1)
            expert_parts = lax.dynamic_update_slice_in_dim(
                jnp.zeros((NFFN * 3,), f32),
                jnp.sum(expert_x * expert_x, axis=(2, 3)).reshape(-1),
                s * local_experts * 3,
                0,
            )
            return jnp.concatenate(
                [
                    jnp.sum(attention_x * attention_x, axis=(1, 2)),
                    vector_parts[0:2],
                    jnp.sum(vector_parts[2:4])[None],
                    jnp.sum(vector_parts[4:])[None],
                    expert_parts,
                ]
            )

        count = 8 + 3 * NFFN
        small = jnp.concatenate(
            [
                squares(attention_master, vector_master, expert_master),
                squares(attention_u, vector_u, expert_u),
                dmixing.reshape(-1),
            ]
        )
        used = small.shape[0]
        small = jnp.pad(small, (0, -used % 128)).reshape(-1, 128)
        small = sum_everywhere(small, sizes).reshape(-1)
        summed_squares = small[: 2 * count].reshape(2, count)
        mixing_grad = small[2 * count : used].reshape(NEXP, NEXP)
        mixing_m, mixing_s, mixing_u = moments(
            mixing_master, mixing_first, mixing_second, mixing_grad
        )
        mixing_squares = jnp.stack(
            [jnp.sum(mixing_master * mixing_master), jnp.sum(mixing_u * mixing_u)]
        )
        tensor_norms = jnp.sqrt(jnp.concatenate([summed_squares, mixing_squares[:, None]], axis=1))
        ratios = learn_rate * (tensor_norms[0] / (tensor_norms[1] + norm_eps))
        vector_ratio = jnp.concatenate(
            [
                ratios[4:6],
                jnp.broadcast_to(ratios[6:7], (2,)),
                jnp.broadcast_to(ratios[7:8], (NEXP,)),
            ]
        )[:, None]
        expert_ratio = lax.dynamic_slice_in_dim(
            ratios[8:count].reshape(NFFN, 3), s * local_experts, local_experts, 0
        )[:, :, None, None]
        return (
            block_output[None],
            input_gradient[None],
            attention_master - ratios[0:4][:, None, None] * attention_u,
            vector_master - vector_ratio * vector_u,
            expert_master - expert_ratio * expert_u,
            mixing_master - ratios[count] * mixing_u,
            attention_m,
            vector_m,
            expert_m,
            mixing_m,
            attention_s,
            vector_s,
            expert_s,
            mixing_s,
            tensor_norms,
        )

    return shards


def solution(mesh):
    n_dp, n_seq, n_shard = (mesh.shape[name] for name in ("dp", "seq", "shard"))
    finer = jax.sharding.Mesh(
        mesh.devices.reshape(n_dp // 2, 2, n_seq, n_shard // 2, 2), DP + ("seq",) + SHARD
    )
    tokens_spec = P(DP + SHARD, "seq", None)
    attention_spec = P(None, DP + ("seq",) + SHARD, None)
    vector_spec = P(None, DP + ("seq",) + SHARD)
    expert_spec = P(SHARD, None, DP + ("seq",), None)
    weights = (attention_spec, vector_spec, expert_spec, P())
    return jax.shard_map(
        make_shards(dict(finer.shape)),
        mesh=finer,
        in_specs=(tokens_spec,) * 5 + weights * 3,
        out_specs=(tokens_spec,) * 2 + weights * 3 + (P(),),
        check_vma=False,
    )
```

```python
import jax
import jax.numpy as jnp
import numpy as np
from jax import lax
from jax.experimental import pallas as pl
from jax.experimental.layout import Layout, with_layout_constraint
from jax.experimental.pallas import tpu as pltpu
from jax.sharding import PartitionSpec as P

HEADS = 12
HDIM = 64
NFFN = 8
TOP = 2
STEP = 4
NEXP = 12

beta_one = 0.9
beta_two = 0.999
adam_eps = 1e-06
weight_decay = 0.01
learn_rate = 0.25
norm_eps = 1e-06
rope_base = 10000.0

bf16 = jnp.bfloat16
f32 = jnp.float32


def exact_dot(left, right):
    return jnp.dot(left, right, precision=lax.Precision.HIGHEST, preferred_element_type=f32)


def dot_nn(left, right):
    return lax.dot_general(left, right, (((1,), (0,)), ((), ())), preferred_element_type=f32)


def dot_nt(left, right):
    return lax.dot_general(left, right, (((1,), (1,)), ((), ())), preferred_element_type=f32)


def dot_tn(left, right):
    return lax.dot_general(left, right, (((0,), (0,)), ((), ())), preferred_element_type=f32)


def rotary_tables(length):
    freqs = np.float32(rope_base) ** (-np.arange(0, HDIM, 2).astype(np.float32) / np.float32(HDIM))
    angles = np.arange(length).astype(np.float32)[:, None] * freqs[None, :]
    cosine = np.cos(angles.astype(np.float64)).astype(np.float32)
    sine = np.sin(angles.astype(np.float64)).astype(np.float32)
    return (
        jnp.asarray(np.concatenate([cosine] * 4, axis=-1)),
        jnp.asarray(np.concatenate([-sine, sine, -sine, sine], axis=-1)),
    )


def softmax_rows(logits):
    row_top = jnp.max(logits, axis=-1, keepdims=True)
    expd_values = jnp.exp(logits - row_top)
    return expd_values / jnp.sum(expd_values, axis=-1, keepdims=True)


def moments(weight, first, second, grad):
    first_new = beta_one * first + (1.0 - beta_one) * grad
    second_new = beta_two * second + (1.0 - beta_two) * grad * grad
    step_value = (
        first_new
        / (1.0 - beta_one**STEP)
        / (jnp.sqrt(second_new / (1.0 - beta_two**STEP)) + adam_eps)
        + weight_decay * weight
    )
    return (first_new, second_new, step_value)


DP = ("dp_far", "dp_near")
SHARD = ("x", "core")


def after(value, *others):
    return lax.optimization_barrier((value,) + others)[0]


def swap(value, axis_name):
    return lax.ppermute(value, axis_name, [(0, 1), (1, 0)])


def swap_seq(value):
    return swap(value, "seq")


def in_order(own, other, which, axis):
    low = jnp.where(which == 0, own, other)
    high = jnp.where(which == 0, other, own)
    return jnp.concatenate([low, high], axis=axis)


def gather_steps(value, axis_name, place, count):
    out = jnp.zeros((count,) + value.shape, value.dtype)
    out = lax.dynamic_update_index_in_dim(out, value, place, 0)
    for step in range(1, count):
        got = lax.ppermute(value, axis_name, [(i, (i + step) % count) for i in range(count)])
        out = lax.dynamic_update_index_in_dim(out, got, (place - step) % count, 0)
    return out


def scatter_steps(value, axis_name, place, count):
    total = lax.dynamic_index_in_dim(value, place, 0, keepdims=False).astype(f32)
    got = []
    for step in range(1, count):
        block = lax.dynamic_index_in_dim(value, (place + step) % count, 0, keepdims=False)
        got.append(lax.ppermute(block, axis_name, [(i, (i + step) % count) for i in range(count)]))
    for part in got:
        total = total + part.astype(f32)
    return total


def keep_and_send(value, place, axis):
    return (
        lax.dynamic_index_in_dim(value, place, axis, keepdims=False),
        lax.dynamic_index_in_dim(value, 1 - place, axis, keepdims=False),
    )


def sum_everywhere(value, sizes):
    for axis_names in (("core",), ("seq", "x"), DP):
        count = 1
        for name in axis_names:
            count *= sizes[name]
        rounds = [[1 << bit] for bit in range(count.bit_length() - 1)]
        if count <= 4:
            rounds = [range(1, count)]
        for steps in rounds:
            got = [
                lax.ppermute(value, axis_names, [(i, i ^ step) for i in range(count)])
                for step in steps
            ]
            if len(got) == 3:
                value = (value + got[0]) + (got[1] + got[2])
            else:
                value = value + got[0]
    return value


QUERY_ROWS = 256
FF_COLUMNS = 512

def turn(value):
    lane = lax.broadcasted_iota(jnp.int32, value.shape, 1) % HDIM
    return jnp.where(lane < HDIM // 2, pltpu.roll(value, 96, 1), pltpu.roll(value, 32, 1))

def attention_forward_kernel(x_ref, gain_ref, wq_ref, wk_ref, wv_ref, cos_ref, sin_ref, h_ref, q_ref, k_ref, v_ref, o_ref, lse_ref):
    length = x_ref.shape[0]

    @pl.when(pl.program_id(0) == 0)
    def _():
        for start in range(0, length, QUERY_ROWS):
            rows = pl.ds(start, QUERY_ROWS)
            x = x_ref[rows, :].astype(f32)
            rho = lax.rsqrt(jnp.mean(x * x, axis=-1, keepdims=True) + norm_eps)
            h_ref[rows, :] = (x * rho * gain_ref[...]).astype(bf16)

    for start in range(0, length, QUERY_ROWS):
        rows = pl.ds(start, QUERY_ROWS)
        h = h_ref[rows, :]
        cos, sin = cos_ref[rows, :], sin_ref[rows, :]
        q = dot_nn(h, wq_ref[...])
        k = dot_nn(h, wk_ref[...])
        q_ref[rows, :] = (q * cos + turn(q) * sin).astype(bf16)
        k_ref[rows, :] = (k * cos + turn(k) * sin).astype(bf16)
        v_ref[rows, :] = dot_nn(h, wv_ref[...]).astype(bf16)

    ahead = lax.broadcasted_iota(jnp.int32, (QUERY_ROWS, QUERY_ROWS), 1) > lax.broadcasted_iota(jnp.int32, (QUERY_ROWS, QUERY_ROWS), 0)
    for start in range(0, length, QUERY_ROWS):
        end = start + QUERY_ROWS
        outs = []
        for head in range(2):
            lanes = slice(head * HDIM, (head + 1) * HDIM)
            q = q_ref[start:end, lanes]
            s = dot_nt(q, k_ref[:end, lanes]) * (HDIM**-0.5)
            last = jnp.where(ahead, -1e30, s[:, start:])
            s = jnp.concatenate([s[:, :start], last], axis=1) if start else last
            top = jnp.max(s, axis=-1, keepdims=True)
            p = jnp.exp(s - top)
            total = jnp.sum(p, axis=-1, keepdims=True)
            p = (p * (1.0 / total)).astype(bf16)
            outs.append(dot_nn(p, v_ref[:end, lanes]))
            lse = jnp.broadcast_to(top + jnp.log(total), (QUERY_ROWS, 128))
            lse_ref[0, head : head + 1, start:end] = lse.T[0:1, :]
        o_ref[start:end, :] = jnp.concatenate(outs, axis=1).astype(bf16)

def attention_forward(x, gain, weight, cos, sin):
    length, width = x.shape
    half = weight.shape[1] // 3
    pairs = half // 128
    full = lambda shape: pl.BlockSpec(shape, lambda p: (0,) * len(shape))
    col = lambda base: pl.BlockSpec((width, 128), lambda p, base=base: (0, base + p))
    out_col = pl.BlockSpec((length, 128), lambda p: (0, p))
    return pl.pallas_call(
        attention_forward_kernel,
        grid=(pairs,),
        in_specs=[full((length, width)), full((1, width)), col(0), col(pairs), col(2 * pairs), full((length, 128)), full((length, 128))],
        out_specs=[full((length, width)), out_col, out_col, out_col, out_col, pl.BlockSpec((1, 2, length), lambda p: (p, 0, 0))],
        out_shape=[jax.ShapeDtypeStruct((length, width), bf16)] + [jax.ShapeDtypeStruct((length, half), bf16)] * 4 + [jax.ShapeDtypeStruct((pairs, 2, length), f32)],
        compiler_params=pltpu.CompilerParams(vmem_limit_bytes=40 * 2**20),
        cost_estimate=pl.CostEstimate(flops=6 * length * width * half + 4 * length * length * half, bytes_accessed=8 * length * width, transcendentals=length * length * half // HDIM),
    )(x, gain, weight, weight, weight, cos, sin)

def attention_backward_kernel(h_ref, x_ref, vector_ref, q_ref, k_ref, v_ref, do_ref, lse_ref, wq_ref, wk_ref, wv_ref, cos_ref, sin_ref, dw_ref, dh_ref, dq_scr, dk_scr, dv_scr):
    length = h_ref.shape[0]
    step = pl.program_id(0)
    behind = lax.broadcasted_iota(jnp.int32, (QUERY_ROWS, QUERY_ROWS), 0) > lax.broadcasted_iota(jnp.int32, (QUERY_ROWS, QUERY_ROWS), 1)
    dk_scr[...] = jnp.zeros_like(dk_scr)
    dv_scr[...] = jnp.zeros_like(dv_scr)
    for start in range(0, length, QUERY_ROWS):
        end = start + QUERY_ROWS
        for head in range(2):
            lanes = slice(head * HDIM, (head + 1) * HDIM)
            q, do = q_ref[start:end, lanes], do_ref[start:end, lanes]
            k, v = k_ref[:end, lanes], v_ref[:end, lanes]
            s = dot_nt(k, q) * (HDIM**-0.5) - lse_ref[0, head : head + 1, start:end]
            last = jnp.where(behind, -1e30, s[start:])
            s = jnp.concatenate([s[:start], last], axis=0) if start else last
            p = jnp.exp(s)
            dp = dot_nt(v, do)
            delta = jnp.sum(p * dp, axis=0, keepdims=True)
            ds = (p * (dp - delta)).astype(bf16)
            dq_scr[start:end, lanes] = dot_tn(ds, k) * (HDIM**-0.5)
            dk_scr[:end, lanes] += dot_nn(ds, q)
            dv_scr[:end, lanes] += dot_nn(p.astype(bf16), do)
    cos, sin = cos_ref[...], sin_ref[...]

    dq = dq_scr[...].astype(bf16).astype(f32)
    dk = (dk_scr[...] * (HDIM**-0.5)).astype(bf16).astype(f32)
    dqp = (dq * cos + turn(dq * sin)).astype(bf16)
    dkp = (dk * cos + turn(dk * sin)).astype(bf16)
    dvb = dv_scr[...].astype(bf16)
    d = jnp.concatenate([dqp, dkp, dvb], axis=1)
    w = jnp.concatenate([wq_ref[...], wk_ref[...], wv_ref[...]], axis=1)
    columns = d.shape[1]
    place = pl.ds(pl.multiple_of(step * columns, 128), columns)
    dw_ref[:, place] = dot_tn(h_ref[...], d).astype(bf16)
    dh = dot_nt(d, w)

    @pl.when(step == 0)
    def _():
        dh_ref[...] = dh

    @pl.when(step > 0)
    def _():
        dh_ref[...] += dh

    @pl.when(step == pl.num_programs(0) - 1)
    def _():
        dgain = jnp.zeros((1, x_ref.shape[1]), f32)
        for start in range(0, length, QUERY_ROWS):
            rows = pl.ds(start, QUERY_ROWS)
            x = x_ref[rows, :].astype(f32)
            rho = lax.rsqrt(jnp.mean(x * x, axis=-1, keepdims=True) + norm_eps)
            dgain += jnp.sum(dh_ref[rows, :] * (x * rho), axis=0, keepdims=True)
        turned = jnp.broadcast_to(dgain, (128, x_ref.shape[1])).T
        lane = lax.broadcasted_iota(jnp.int32, turned.shape, 1)
        vectors = jnp.where(lane == 0, turned, vector_ref[...])
        dw_ref[:, dw_ref.shape[1] - 128 :] = vectors.astype(bf16)

def attention_backward(h, x, vectors, q, k, v, do, lse, weight, cos, sin):
    length, width = h.shape
    half = weight.shape[1] // 3
    pairs = half // 128
    full = lambda shape: pl.BlockSpec(shape, lambda p: (0,) * len(shape))
    col = lambda base: pl.BlockSpec((width, 128), lambda p, base=base: (0, base + p))
    out_col = pl.BlockSpec((length, 128), lambda p: (0, p))
    return pl.pallas_call(
        attention_backward_kernel,
        grid=(pairs,),
        in_specs=[full((length, width)), full((length, width)), full((width, 128)), out_col, out_col, out_col, out_col, pl.BlockSpec((1, 2, length), lambda p: (p, 0, 0)), col(0), col(pairs), col(2 * pairs), full((length, 128)), full((length, 128))],
        out_specs=[full((width, 3 * half + 128)), full((length, width))],
        out_shape=[jax.ShapeDtypeStruct((width, 3 * half + 128), bf16), jax.ShapeDtypeStruct((length, width), f32)],
        scratch_shapes=[pltpu.VMEM((length, 128), f32)] * 3,
        compiler_params=pltpu.CompilerParams(vmem_limit_bytes=48 * 2**20),
        cost_estimate=pl.CostEstimate(flops=12 * length * width * half + 10 * length * length * half, bytes_accessed=12 * length * width, transcendentals=length * length * half // HDIM),
    )(h, x, vectors, q, k, v, do, lse, weight, weight, weight, cos, sin)


def gate_columns(value, which):
    high = lax.reduce_precision(value, 8, 7)
    middle = lax.reduce_precision(value - high, 8, 7)
    low = lax.reduce_precision(value - high - middle, 8, 7)
    lane = lax.broadcasted_iota(jnp.int32, (value.shape[0], 128), 1)
    columns = jnp.where(lane == 3, 1.0 * which, 0.0)
    for part, place in ((high, 0), (middle, 1), (low, 2)):
        columns = jnp.where(lane == place + 4 * which, part, columns)
    return columns.astype(bf16)


def expert_kernel(
    flipped_ref,
    taken_ref,
    dout_ref,
    same_ref,
    other_ref,
    f_ref,
    dtaken_ref,
    gradient_ref,
    weight_ref,
    f_acc,
    d_acc,
    dresult_ref,
    taken_turned,
    dresult_turned,
):
    step, last = pl.program_id(0), pl.num_programs(0) - 1
    width = dout_ref.shape[1]

    @pl.when(step == 0)
    def _():
        lanes = taken_ref[:, width:].astype(f32)
        lane = lax.broadcasted_iota(jnp.int32, lanes.shape, 1)
        gate = jnp.sum(jnp.where(lane == 3, 0.0, lanes), axis=1, keepdims=True)
        dresult_ref[...] = (gate * dout_ref[...].astype(f32)).astype(bf16)
        taken_turned[...] = taken_ref[:, :width].T
        dresult_turned[...] = dresult_ref[...].T

    eighth = width // 8
    shift = flipped_ref[0] * eighth
    for matrix in range(3):
        for pair in range(4):
            rows = slice(pair * eighth, (pair + 1) * eighth)
            base = 2 * pair * eighth
            place = pl.ds(pl.multiple_of(base + shift, 32), eighth)
            weight_ref[matrix, place, :] = same_ref[matrix, rows, :]
            place = pl.ds(pl.multiple_of(base + eighth - shift, 32), eighth)
            weight_ref[matrix, place, :] = other_ref[matrix, rows, :]
    taken = taken_ref[:, :width]
    a = dot_nn(taken, weight_ref[0])
    b = dot_nn(taken, weight_ref[1])
    sig = jax.nn.sigmoid(a)
    act = a * sig
    hidden = (act * b).astype(bf16)
    gradient_ref[2] = dot_nn(dresult_turned[...], hidden).astype(bf16)
    dhidden = dot_nn(dresult_ref[...], weight_ref[2])
    dgate = (dhidden * b * (sig * (1.0 + a - act))).astype(bf16)
    dup = (dhidden * act).astype(bf16)
    gradient_ref[0] = dot_nn(taken_turned[...], dgate).astype(bf16)
    gradient_ref[1] = dot_nn(taken_turned[...], dup).astype(bf16)
    f = dot_nt(hidden, weight_ref[2])
    d = dot_nt(dgate, weight_ref[0]) + dot_nt(dup, weight_ref[1])

    @pl.when(step == 0)
    def _():
        f_acc[...] = f
        d_acc[...] = d

    @pl.when(step > 0)
    def _():
        f_acc[...] += f
        d_acc[...] += d

    @pl.when(step == last)
    def _():
        f = f_acc[...].astype(bf16)
        f_ref[...] = f
        dtaken_ref[:, :width] = d_acc[...].astype(bf16)
        dpicked = jnp.sum(dout_ref[...].astype(f32) * f.astype(f32), axis=1, keepdims=True)
        high = dpicked.astype(bf16).astype(f32)
        middle = (dpicked - high).astype(bf16).astype(f32)
        low = (dpicked - high - middle).astype(bf16).astype(f32)
        lanes = taken_ref[:, width:].astype(f32)
        lane = lax.broadcasted_iota(jnp.int32, lanes.shape, 1)
        second = jnp.sum(jnp.where(lane == 3, lanes, 0.0), axis=1, keepdims=True)
        mine = jnp.where(lane < 3, 1.0 - second, jnp.where((lane > 3) & (lane < 7), second, 0.0))
        part = jnp.where(lane % 4 == 0, high, jnp.where(lane % 4 == 1, middle, low))
        dtaken_ref[:, width:] = (mine * part).astype(bf16)


def expert_compute(flipped, taken, dout, same, other):
    rows, width = dout.shape
    hidden = same.shape[2]
    half = pl.BlockSpec((3, width // 2, FF_COLUMNS), lambda i: (0, 0, i))
    whole = lambda columns: pl.BlockSpec((rows, columns), lambda i: (0, 0))
    shape = lambda columns: jax.ShapeDtypeStruct((rows, columns), bf16)
    return pl.pallas_call(
        expert_kernel,
        grid=(hidden // FF_COLUMNS,),
        in_specs=[
            pl.BlockSpec(memory_space=pltpu.SMEM),
            whole(width + 128),
            whole(width),
            half,
            half,
        ],
        out_specs=[
            whole(width),
            whole(width + 128),
            pl.BlockSpec((3, width, FF_COLUMNS), lambda i: (0, 0, i)),
        ],
        out_shape=[
            shape(width),
            shape(width + 128),
            jax.ShapeDtypeStruct((3, width, hidden), bf16),
        ],
        scratch_shapes=[pltpu.VMEM((3, width, FF_COLUMNS), bf16)]
        + [pltpu.VMEM((rows, width), f32)] * 2
        + [pltpu.VMEM((rows, width), bf16)]
        + [pltpu.VMEM((width, rows), bf16)] * 2,
        compiler_params=pltpu.CompilerParams(vmem_limit_bytes=58 * 2**20),
        cost_estimate=pl.CostEstimate(
            flops=20 * rows * width * hidden,
            bytes_accessed=6 * width * hidden + 6 * rows * hidden,
            transcendentals=rows * hidden,
        ),
    )(flipped, taken, dout, same, other)


def make_shards(sizes):
    n_seq, n_x = sizes["seq"], sizes["x"]
    n_dp = sizes["dp_far"] * sizes["dp_near"]

    def shards(
        tokens,
        cotangent,
        previous_logits,
        routes,
        priority,
        attention_master,
        vector_master,
        expert_master,
        mixing_master,
        attention_first,
        vector_first,
        expert_first,
        mixing_first,
        attention_second,
        vector_second,
        expert_second,
        mixing_second,
    ):
        z, y, s = lax.axis_index(DP), lax.axis_index("seq"), lax.axis_index(SHARD)
        far, near = lax.axis_index("dp_far"), lax.axis_index("dp_near")
        x_place, core = lax.axis_index("x"), lax.axis_index("core")
        row_count, model_width = tokens.shape[1], tokens.shape[2]
        half_width = model_width // 2
        local_experts = expert_master.shape[0]
        spread = local_experts == 2 and n_x == 2 and sizes["dp_far"] == 2
        ep_axes = ("dp_near", "seq", "x") if spread else SHARD
        ep_place = lax.axis_index(ep_axes)
        own_rows = attention_master.shape[1]

        def cross(same_y, other_y):
            got = lax.ppermute(same_y, ("dp_near", "core"), [(1, 2), (2, 1)])
            moves = [
                (4 * n + 2 * q + c, 4 * c + 2 * (1 - q) + n)
                for n in range(2)
                for q in range(2)
                for c in range(2)
            ]
            return (
                jnp.where(near == core, same_y, got),
                lax.ppermute(other_y, ("dp_near", "seq", "core"), moves),
            )

        attention_low = attention_master.astype(bf16)
        vector_low = vector_master.astype(bf16).T
        vector_pad = 128 - vector_low.shape[1]

        def weight_pack(which):
            columns = lax.dynamic_slice_in_dim(attention_low[:3], which * half_width, half_width, 2)
            return jnp.concatenate(
                [columns[0], columns[1], columns[2], attention_low[3], jnp.pad(vector_low, ((0, 0), (0, vector_pad)))],
                axis=1,
            )

        packed = in_order(weight_pack(y)[None], swap_seq(weight_pack(1 - y))[None], y, 0)

        packed_z = gather_steps(packed, DP, z, n_dp)
        packed_x = gather_steps(packed_z, "x", x_place, n_x)
        expert_low = after(expert_master, packed).astype(bf16)
        if spread:
            same_y, other_y = cross(*keep_and_send(expert_low, y, 0))
            expert_same = lax.all_gather(
                after(same_y, packed_z), ("dp_far", "core"), axis=1, tiled=True
            )
            expert_other = lax.all_gather(
                after(other_y, packed_z), ("dp_far", "core"), axis=1, tiled=True
            )
            flipped = y
        else:
            expert_use = lax.all_gather(expert_low[0], DP + ("seq",), axis=1, tiled=True)
            expert_use = expert_use.reshape(3, 4, 2, model_width // 8, -1)
            expert_same = expert_use[:, :, 0].reshape(3, model_width // 2, -1)
            expert_other = expert_use[:, :, 1].reshape(3, model_width // 2, -1)
            flipped = jnp.zeros_like(y)

        packed = packed_x
        packed = in_order(packed[None], swap(packed, "core")[None], core, 0)
        packed = packed.transpose(2, 3, 1, 0, 4, 5).reshape(model_width, -1)
        qkv_weight = packed[:, : 3 * half_width]
        out_weight = packed[:, 3 * half_width : 3 * half_width + model_width]
        vector_all = packed[:, 3 * half_width + model_width :][:, : 4 + NEXP].T

        route_rows = routes[0]
        order = priority[0, 0]
        capacity = 9 * row_count * TOP // (8 * NEXP)
        expert_ids = jnp.arange(NEXP)[None, :]
        hit_each = [route_rows[:, j : j + 1] == expert_ids for j in range(TOP)]
        hits = (hit_each[0] | hit_each[1]).astype(bf16)
        before = (order[None, :] < order[:, None]).astype(bf16)
        counts = dot_nn(before, hits)
        kept, dispatch = [], []
        block_ids = jnp.arange(NFFN * capacity)[None, :]
        for j in range(TOP):
            slot = jnp.sum(jnp.where(hit_each[j], counts, 0.0), axis=1, keepdims=True).astype(
                jnp.int32
            )
            route = route_rows[:, j : j + 1]
            keep = (route < NFFN) & (slot < capacity)
            block = ((route // 2) % 2) * 4 + (route % 2) * 2 + route // 4 if spread else route
            block = block ^ ep_place
            kept.append(keep)
            dispatch.append(
                ((block_ids == block * capacity + slot) & keep).astype(bf16)
            )
        dispatch_both = dispatch[0] + dispatch[1]

        tokens_all = in_order(tokens[0], swap_seq(tokens[0]), y, 0)
        gain_one = vector_all[0].astype(f32)[None, :]
        gain_two = vector_all[1].astype(f32)[None, :]
        cosine, sine = rotary_tables(tokens_all.shape[0])
        normed, query, key, value, mixed, log_sums = attention_forward(
            tokens_all, gain_one, qkv_weight, cosine, sine
        )

        upstream = cotangent[0].astype(f32)
        def exchange(rows):
            blocks = rows.reshape(NFFN, capacity, rows.shape[1])
            return [blocks[0]] + [
                lax.ppermute(blocks[k], ep_axes, [(i, i ^ k) for i in range(NFFN)])
                for k in range(1, NFFN)
            ]

        def exchanged(rows):
            return jnp.concatenate(exchange(rows), axis=0)

        dout_rows = dot_tn(dispatch_both, cotangent[0]).astype(bf16)
        dout_rows = exchange(after(dout_rows, tokens_all))
        mixed, dout_rows = lax.optimization_barrier((mixed, dout_rows))

        mixed_keep = lax.dynamic_slice_in_dim(mixed, y * row_count, row_count, 0)
        mixed_send = lax.dynamic_slice_in_dim(mixed, (1 - y) * row_count, row_count, 0)
        mixed_tokens = in_order(mixed_keep, swap_seq(mixed_send), y, 1)

        inputs = tokens[0].astype(f32)
        resid = inputs + dot_nn(mixed_tokens, out_weight)
        rho_two = lax.rsqrt(jnp.mean(resid * resid, axis=-1, keepdims=True) + norm_eps)
        normed_two = resid * rho_two * gain_two
        expert_in = normed_two.astype(bf16)
        router = vector_all[4:]
        previous = previous_logits[0]
        logits = dot_nt(expert_in, router) + exact_dot(previous, mixing_master)
        gates = softmax_rows(logits)
        picked = [
            jnp.sum(jnp.where(hit_each[j], gates, 0.0), axis=1, keepdims=True) for j in range(TOP)
        ]

        consts = vector_all[2:4].astype(f32)
        dlocal = [
            jnp.sum(upstream * normed_two, axis=-1, keepdims=True),
            jnp.sum(upstream * consts[0:1], axis=-1, keepdims=True),
            jnp.sum(upstream * consts[1:2], axis=-1, keepdims=True),
        ]

        taken = dot_tn(
            jnp.concatenate(dispatch, axis=0),
            jnp.concatenate(
                [
                    jnp.concatenate([expert_in, gate_columns(picked[j], j)], axis=1)
                    for j in range(TOP)
                ],
                axis=0,
            ),
        ).astype(bf16)
        taken = exchanged(taken)
        dout_rows = jnp.concatenate(dout_rows, axis=0)
        result, dtaken, dexpert = expert_compute(
            flipped[None].astype(jnp.int32), taken, dout_rows, expert_same, expert_other
        )
        dtaken = exchange(dtaken)
        dtaken = jnp.concatenate(dtaken, axis=0)

        def sum_rows(grad):
            axes = ("dp_far", "core") if spread else DP + ("seq",)
            return lax.psum_scatter(grad, axes, scatter_dimension=1, tiled=True)

        def to_owners(same_y, other_y):
            if not spread:
                return same_y[None]
            same_y, other_y = cross(same_y, other_y)
            return in_order(same_y[None], other_y[None], y, 0)

        result = exchange(after(result, dtaken))
        dexpert = sum_rows(dexpert)
        if spread:
            row_parts = keep_and_send(dexpert.reshape(3, 2, -1, dexpert.shape[2]), y, 1)
        else:
            row_parts = (dexpert, dexpert)


        dgates = jnp.zeros_like(gates)
        returned = dot_nn(dispatch_both, dtaken)
        dnormed_two = returned[:, :model_width]
        value_weight = [0.0, 0.0, 0.0]
        for j in range(TOP):
            route = route_rows[:, j : j + 1]
            local = [jnp.where(route == NFFN + 1 + i, 1.0, 0.0) for i in range(3)]
            parts = returned[:, model_width + 4 * j : model_width + 4 * j + 3]
            dpicked = jnp.sum(parts, axis=1, keepdims=True)
            for i in range(3):
                dpicked = dpicked + jnp.where(route == NFFN + 1 + i, dlocal[i], 0.0)
                value_weight[i] = value_weight[i] + local[i] * picked[j]
            dgates = dgates + jnp.where(hit_each[j], dpicked, 0.0)
        dnormed_two = dnormed_two + value_weight[0] * upstream
        dconst_one = jnp.sum(value_weight[1] * upstream, axis=0, keepdims=True)
        dconst_two = jnp.sum(value_weight[2] * upstream, axis=0, keepdims=True)
        dlogits = gates * (dgates - jnp.sum(gates * dgates, axis=-1, keepdims=True))
        dnormed_two = dnormed_two + exact_dot(dlogits, router.astype(f32))
        drouter = exact_dot(dlogits.T, expert_in.astype(f32))
        dmixing = exact_dot(previous.T, dlogits)
        scaled_two = dnormed_two * gain_two
        dresid = upstream + (
            rho_two * scaled_two
            - resid * (rho_two * rho_two * rho_two) * jnp.mean(resid * scaled_two, -1, keepdims=True)
        )
        dgain_two = jnp.sum(dnormed_two * resid * rho_two, axis=0, keepdims=True)
        dbranch_low = dresid.astype(bf16)
        dweight_out = dot_tn(mixed_tokens, dbranch_low)

        group, place = n_seq * n_x, y * n_x + x_place

        def core_sum(grad):
            grad = grad.astype(bf16).reshape(n_dp, n_seq, n_x, 2, own_rows, -1)
            keep, send = keep_and_send(grad.transpose(3, 1, 2, 0, 4, 5), core, 0)
            return (keep.astype(f32) + swap(send, "core").astype(f32)).astype(bf16)

        def plane_sum(grad):
            grad = grad.reshape((group,) + grad.shape[2:])
            totals = [lax.dynamic_index_in_dim(grad, place, 0, keepdims=False).astype(f32), 0.0]
            for step in range(1, group):
                block = lax.dynamic_index_in_dim(grad, place ^ step, 0, keepdims=False)
                got = lax.ppermute(block, ("seq", "x"), [(i, i ^ step) for i in range(group)])
                totals[step // n_x] = totals[step // n_x] + got.astype(f32)
            return totals

        def dp_sum(grad, wait_for):
            return scatter_steps(after(grad.astype(bf16), wait_for), DP, z, n_dp)

        dmixed = dot_nt(dbranch_low, out_weight).astype(bf16)
        dmixed_keep = lax.dynamic_slice_in_dim(dmixed, y * half_width, half_width, 1)
        dmixed_send = lax.dynamic_slice_in_dim(dmixed, (1 - y) * half_width, half_width, 1)
        dmixed_heads = in_order(dmixed_keep, swap_seq(dmixed_send), y, 0)
        dout_part = core_sum(dweight_out)
        vectors = jnp.concatenate(
            [jnp.zeros_like(dgain_two), dgain_two, dconst_one, dconst_two, drouter], axis=0
        )
        vectors = jnp.pad(vectors.T, ((0, 0), (0, vector_pad)))
        dpack, dnormed_all = attention_backward(
            normed, tokens_all, vectors, query, key, value, dmixed_heads, log_sums, qkv_weight, cosine, sine
        )
        dpack, result = after((dpack, result), dnormed_all)
        dpack = after(dpack, result)
        this_y, other_y = plane_sum(jnp.concatenate([core_sum(dpack), dout_part], axis=-1))
        columns = 3 * half_width
        dpack = dp_sum(
            (
                jnp.concatenate(
                    [
                        this_y[..., :columns],
                        other_y[..., :columns],
                        this_y[..., columns:] + other_y[..., columns:],
                    ],
                    axis=-1,
                ).astype(bf16)
            ),
            row_parts,
        )
        dnormed_keep = lax.dynamic_slice_in_dim(dnormed_all, y * row_count, row_count, 0)
        dnormed_send = lax.dynamic_slice_in_dim(
            after(dnormed_all, this_y), (1 - y) * row_count, row_count, 0
        )
        dnormed = dnormed_keep + swap_seq(dnormed_send.astype(bf16)).astype(f32)
        rho_one = lax.rsqrt(jnp.mean(inputs * inputs, axis=-1, keepdims=True) + norm_eps)
        scaled_one = dnormed * gain_one
        input_gradient = dresid + (
            rho_one * scaled_one
            - inputs * (rho_one * rho_one * rho_one) * jnp.mean(inputs * scaled_one, -1, keepdims=True)
        )
        dpack = after(dpack, dexpert)
        result = jnp.concatenate(result, axis=0)
        mixture = (
            picked[0] * dot_nn(dispatch[0], result)
            + picked[1] * dot_nn(dispatch[1], result)
            + value_weight[0] * normed_two
            + value_weight[1] * consts[0:1]
            + value_weight[2] * consts[1:2]
        )
        block_output = (resid + mixture).astype(bf16)
        dpack = with_layout_constraint(dpack, Layout((0, 1)))
        head_pairs = half_width // 128

        def by_matrix(part):
            return jnp.stack(
                [
                    jnp.concatenate(
                        [
                            part[:, 384 * pair + 128 * which : 384 * pair + 128 * which + 128]
                            for pair in range(head_pairs)
                        ],
                        axis=1,
                    )
                    for which in range(3)
                ]
            )

        qkv_sum = in_order(
            by_matrix(dpack[:, :columns]), by_matrix(dpack[:, columns : 2 * columns]), y, 2
        )
        vector_sum = dpack[:, 2 * columns :][:, : 4 + NEXP].T
        dout_sum = dpack[:, 2 * columns + 128 :]
        attention_sum = jnp.concatenate([qkv_sum, dout_sum[None]], axis=0)

        attention_m, attention_s, attention_u = moments(
            attention_master, attention_first, attention_second, attention_sum
        )
        vector_m, vector_s, vector_u = moments(
            vector_master, vector_first, vector_second, vector_sum
        )
        expert_sum = to_owners(*row_parts).astype(f32)
        expert_m, expert_s, expert_u = moments(
            expert_master, expert_first, expert_second, expert_sum
        )

        expert_u = lax.optimization_barrier(expert_u)

        def squares(attention_x, vector_x, expert_x):
            vector_parts = jnp.sum(vector_x * vector_x, axis=1)
            expert_parts = lax.dynamic_update_slice_in_dim(
                jnp.zeros((NFFN * 3,), f32),
                jnp.sum(expert_x * expert_x, axis=(2, 3)).reshape(-1),
                s * local_experts * 3,
                0,
            )
            return jnp.concatenate(
                [
                    jnp.sum(attention_x * attention_x, axis=(1, 2)),
                    vector_parts[0:2],
                    jnp.sum(vector_parts[2:4])[None],
                    jnp.sum(vector_parts[4:])[None],
                    expert_parts,
                ]
            )

        count = 8 + 3 * NFFN
        small = jnp.concatenate(
            [
                squares(attention_master, vector_master, expert_master),
                squares(attention_u, vector_u, expert_u),
                dmixing.reshape(-1),
            ]
        )
        used = small.shape[0]
        small = jnp.pad(small, (0, -used % 128)).reshape(-1, 128)
        small = sum_everywhere(small, sizes).reshape(-1)
        summed_squares = small[: 2 * count].reshape(2, count)
        mixing_grad = small[2 * count : used].reshape(NEXP, NEXP)
        mixing_m, mixing_s, mixing_u = moments(
            mixing_master, mixing_first, mixing_second, mixing_grad
        )
        mixing_squares = jnp.stack(
            [jnp.sum(mixing_master * mixing_master), jnp.sum(mixing_u * mixing_u)]
        )
        tensor_norms = jnp.sqrt(jnp.concatenate([summed_squares, mixing_squares[:, None]], axis=1))
        ratios = learn_rate * (tensor_norms[0] / (tensor_norms[1] + norm_eps))
        vector_ratio = jnp.concatenate(
            [
                ratios[4:6],
                jnp.broadcast_to(ratios[6:7], (2,)),
                jnp.broadcast_to(ratios[7:8], (NEXP,)),
            ]
        )[:, None]
        expert_ratio = lax.dynamic_slice_in_dim(
            ratios[8:count].reshape(NFFN, 3), s * local_experts, local_experts, 0
        )[:, :, None, None]
        return (
            block_output[None],
            input_gradient[None],
            attention_master - ratios[0:4][:, None, None] * attention_u,
            vector_master - vector_ratio * vector_u,
            expert_master - expert_ratio * expert_u,
            mixing_master - ratios[count] * mixing_u,
            attention_m,
            vector_m,
            expert_m,
            mixing_m,
            attention_s,
            vector_s,
            expert_s,
            mixing_s,
            tensor_norms,
        )

    return shards


def solution(mesh):
    n_dp, n_seq, n_shard = (mesh.shape[name] for name in ("dp", "seq", "shard"))
    finer = jax.sharding.Mesh(
        mesh.devices.reshape(n_dp // 2, 2, n_seq, n_shard // 2, 2), DP + ("seq",) + SHARD
    )
    tokens_spec = P(DP + SHARD, "seq", None)
    attention_spec = P(None, DP + ("seq",) + SHARD, None)
    vector_spec = P(None, DP + ("seq",) + SHARD)
    expert_spec = P(SHARD, None, DP + ("seq",), None)
    weights = (attention_spec, vector_spec, expert_spec, P())
    return jax.shard_map(
        make_shards(dict(finer.shape)),
        mesh=finer,
        in_specs=(tokens_spec,) * 5 + weights * 3,
        out_specs=(tokens_spec,) * 2 + weights * 3 + (P(),),
        check_vma=False,
    )
```

```python
import jax
import jax.numpy as jnp
import numpy as np
from jax import lax
from jax.experimental import pallas as pl
from jax.experimental.layout import Layout, with_layout_constraint
from jax.experimental.pallas import tpu as pltpu
from jax.sharding import PartitionSpec as P

HEADS = 12
HDIM = 64
NFFN = 8
TOP = 2
STEP = 4
NEXP = 12

beta_one = 0.9
beta_two = 0.999
adam_eps = 1e-06
weight_decay = 0.01
learn_rate = 0.25
norm_eps = 1e-06
rope_base = 10000.0

bf16 = jnp.bfloat16
f32 = jnp.float32


def exact_dot(left, right):
    return jnp.dot(left, right, precision=lax.Precision.HIGHEST, preferred_element_type=f32)


def dot_nn(left, right):
    return lax.dot_general(left, right, (((1,), (0,)), ((), ())), preferred_element_type=f32)


def dot_nt(left, right):
    return lax.dot_general(left, right, (((1,), (1,)), ((), ())), preferred_element_type=f32)


def dot_tn(left, right):
    return lax.dot_general(left, right, (((0,), (0,)), ((), ())), preferred_element_type=f32)


def rotary_tables(length):
    freqs = np.float32(rope_base) ** (-np.arange(0, HDIM, 2).astype(np.float32) / np.float32(HDIM))
    angles = np.arange(length).astype(np.float32)[:, None] * freqs[None, :]
    cosine = np.cos(angles.astype(np.float64)).astype(np.float32)
    sine = np.sin(angles.astype(np.float64)).astype(np.float32)
    return (
        jnp.asarray(np.concatenate([cosine] * 4, axis=-1)),
        jnp.asarray(np.concatenate([-sine, sine, -sine, sine], axis=-1)),
    )


def softmax_rows(logits):
    row_top = jnp.max(logits, axis=-1, keepdims=True)
    expd_values = jnp.exp(logits - row_top)
    return expd_values / jnp.sum(expd_values, axis=-1, keepdims=True)


def moments(weight, first, second, grad):
    first_new = beta_one * first + (1.0 - beta_one) * grad
    second_new = beta_two * second + (1.0 - beta_two) * grad * grad
    step_value = (
        first_new
        / (1.0 - beta_one**STEP)
        / (jnp.sqrt(second_new / (1.0 - beta_two**STEP)) + adam_eps)
        + weight_decay * weight
    )
    return (first_new, second_new, step_value)


DP = ("dp_far", "dp_near")
SHARD = ("x", "core")


def after(value, *others):
    return lax.optimization_barrier((value,) + others)[0]


def swap(value, axis_name):
    return lax.ppermute(value, axis_name, [(0, 1), (1, 0)])


def swap_seq(value):
    return swap(value, "seq")


def in_order(own, other, which, axis):
    low = jnp.where(which == 0, own, other)
    high = jnp.where(which == 0, other, own)
    return jnp.concatenate([low, high], axis=axis)


def gather_steps(value, axis_name, place, count):
    out = jnp.zeros((count,) + value.shape, value.dtype)
    out = lax.dynamic_update_index_in_dim(out, value, place, 0)
    for step in range(1, count):
        got = lax.ppermute(value, axis_name, [(i, (i + step) % count) for i in range(count)])
        out = lax.dynamic_update_index_in_dim(out, got, (place - step) % count, 0)
    return out


def scatter_steps(value, axis_name, place, count):
    total = lax.dynamic_index_in_dim(value, place, 0, keepdims=False).astype(f32)
    got = []
    for step in range(1, count):
        block = lax.dynamic_index_in_dim(value, (place + step) % count, 0, keepdims=False)
        got.append(lax.ppermute(block, axis_name, [(i, (i + step) % count) for i in range(count)]))
    for part in got:
        total = total + part.astype(f32)
    return total


def keep_and_send(value, place, axis):
    return (
        lax.dynamic_index_in_dim(value, place, axis, keepdims=False),
        lax.dynamic_index_in_dim(value, 1 - place, axis, keepdims=False),
    )


def sum_everywhere(value, sizes):
    for axis_names in (("core",), ("seq", "x"), DP):
        count = 1
        for name in axis_names:
            count *= sizes[name]
        rounds = [[1 << bit] for bit in range(count.bit_length() - 1)]
        if count <= 4:
            rounds = [range(1, count)]
        for steps in rounds:
            got = [
                lax.ppermute(value, axis_names, [(i, i ^ step) for i in range(count)])
                for step in steps
            ]
            if len(got) == 3:
                value = (value + got[0]) + (got[1] + got[2])
            else:
                value = value + got[0]
    return value


QUERY_ROWS = 256
FF_COLUMNS = 512

def turn(value):
    lane = lax.broadcasted_iota(jnp.int32, value.shape, 1) % HDIM
    return jnp.where(lane < HDIM // 2, pltpu.roll(value, 96, 1), pltpu.roll(value, 32, 1))

def attention_forward_kernel(x_ref, gain_ref, wq_ref, wk_ref, wv_ref, cos_ref, sin_ref, h_ref, q_ref, k_ref, v_ref, o_ref, lse_ref):
    length = x_ref.shape[0]

    @pl.when(pl.program_id(0) == 0)
    def _():
        for start in range(0, length, QUERY_ROWS):
            rows = pl.ds(start, QUERY_ROWS)
            x = x_ref[rows, :].astype(f32)
            rho = lax.rsqrt(jnp.mean(x * x, axis=-1, keepdims=True) + norm_eps)
            h_ref[rows, :] = (x * rho * gain_ref[...]).astype(bf16)

    for start in range(0, length, QUERY_ROWS):
        rows = pl.ds(start, QUERY_ROWS)
        h = h_ref[rows, :]
        cos, sin = cos_ref[rows, :], sin_ref[rows, :]
        q = dot_nn(h, wq_ref[...])
        k = dot_nn(h, wk_ref[...])
        q_ref[rows, :] = (q * cos + turn(q) * sin).astype(bf16)
        k_ref[rows, :] = (k * cos + turn(k) * sin).astype(bf16)
        v_ref[rows, :] = dot_nn(h, wv_ref[...]).astype(bf16)

    ahead = lax.broadcasted_iota(jnp.int32, (QUERY_ROWS, QUERY_ROWS), 1) > lax.broadcasted_iota(jnp.int32, (QUERY_ROWS, QUERY_ROWS), 0)
    for start in range(0, length, QUERY_ROWS):
        end = start + QUERY_ROWS
        outs = []
        for head in range(2):
            lanes = slice(head * HDIM, (head + 1) * HDIM)
            q = q_ref[start:end, lanes]
            s = dot_nt(q, k_ref[:end, lanes]) * (HDIM**-0.5)
            last = jnp.where(ahead, -1e30, s[:, start:])
            s = jnp.concatenate([s[:, :start], last], axis=1) if start else last
            top = jnp.max(s, axis=-1, keepdims=True)
            p = jnp.exp(s - top)
            total = jnp.sum(p, axis=-1, keepdims=True)
            p = (p * (1.0 / total)).astype(bf16)
            outs.append(dot_nn(p, v_ref[:end, lanes]))
            lse = jnp.broadcast_to(top + jnp.log(total), (QUERY_ROWS, 128))
            lse_ref[0, head : head + 1, start:end] = lse.T[0:1, :]
        o_ref[start:end, :] = jnp.concatenate(outs, axis=1).astype(bf16)

def attention_forward(x, gain, weight, cos, sin):
    length, width = x.shape
    half = weight.shape[1] // 3
    pairs = half // 128
    full = lambda shape: pl.BlockSpec(shape, lambda p: (0,) * len(shape))
    col = lambda base: pl.BlockSpec((width, 128), lambda p, base=base: (0, base + p))
    out_col = pl.BlockSpec((length, 128), lambda p: (0, p))
    return pl.pallas_call(
        attention_forward_kernel,
        grid=(pairs,),
        in_specs=[full((length, width)), full((1, width)), col(0), col(pairs), col(2 * pairs), full((length, 128)), full((length, 128))],
        out_specs=[full((length, width)), out_col, out_col, out_col, out_col, pl.BlockSpec((1, 2, length), lambda p: (p, 0, 0))],
        out_shape=[jax.ShapeDtypeStruct((length, width), bf16)] + [jax.ShapeDtypeStruct((length, half), bf16)] * 4 + [jax.ShapeDtypeStruct((pairs, 2, length), f32)],
        compiler_params=pltpu.CompilerParams(vmem_limit_bytes=40 * 2**20),
        cost_estimate=pl.CostEstimate(flops=6 * length * width * half + 4 * length * length * half, bytes_accessed=8 * length * width, transcendentals=length * length * half // HDIM),
    )(x, gain, weight, weight, weight, cos, sin)

def attention_backward_kernel(h_ref, x_ref, vector_ref, q_ref, k_ref, v_ref, do_ref, lse_ref, wq_ref, wk_ref, wv_ref, cos_ref, sin_ref, dw_ref, dh_ref, dq_scr, dk_scr, dv_scr):
    length = h_ref.shape[0]
    step = pl.program_id(0)
    behind = lax.broadcasted_iota(jnp.int32, (QUERY_ROWS, QUERY_ROWS), 0) > lax.broadcasted_iota(jnp.int32, (QUERY_ROWS, QUERY_ROWS), 1)
    dk_scr[...] = jnp.zeros_like(dk_scr)
    dv_scr[...] = jnp.zeros_like(dv_scr)
    for start in range(0, length, QUERY_ROWS):
        end = start + QUERY_ROWS
        for head in range(2):
            lanes = slice(head * HDIM, (head + 1) * HDIM)
            q, do = q_ref[start:end, lanes], do_ref[start:end, lanes]
            k, v = k_ref[:end, lanes], v_ref[:end, lanes]
            s = dot_nt(k, q) * (HDIM**-0.5) - lse_ref[0, head : head + 1, start:end]
            last = jnp.where(behind, -1e30, s[start:])
            s = jnp.concatenate([s[:start], last], axis=0) if start else last
            p = jnp.exp(s)
            dp = dot_nt(v, do)
            delta = jnp.sum(p * dp, axis=0, keepdims=True)
            ds = (p * (dp - delta)).astype(bf16)
            dq_scr[start:end, lanes] = dot_tn(ds, k) * (HDIM**-0.5)
            dk_scr[:end, lanes] += dot_nn(ds, q)
            dv_scr[:end, lanes] += dot_nn(p.astype(bf16), do)
    cos, sin = cos_ref[...], sin_ref[...]

    dq = dq_scr[...].astype(bf16).astype(f32)
    dk = (dk_scr[...] * (HDIM**-0.5)).astype(bf16).astype(f32)
    dqp = (dq * cos + turn(dq * sin)).astype(bf16)
    dkp = (dk * cos + turn(dk * sin)).astype(bf16)
    dvb = dv_scr[...].astype(bf16)
    d = jnp.concatenate([dqp, dkp, dvb], axis=1)
    w = jnp.concatenate([wq_ref[...], wk_ref[...], wv_ref[...]], axis=1)
    columns = d.shape[1]
    place = pl.ds(pl.multiple_of(step * columns, 128), columns)
    dw_ref[:, place] = dot_tn(h_ref[...], d).astype(bf16)
    dh = dot_nt(d, w)

    @pl.when(step == 0)
    def _():
        dh_ref[...] = dh

    @pl.when(step > 0)
    def _():
        dh_ref[...] += dh

    @pl.when(step == pl.num_programs(0) - 1)
    def _():
        dgain = jnp.zeros((1, x_ref.shape[1]), f32)
        for start in range(0, length, QUERY_ROWS):
            rows = pl.ds(start, QUERY_ROWS)
            x = x_ref[rows, :].astype(f32)
            rho = lax.rsqrt(jnp.mean(x * x, axis=-1, keepdims=True) + norm_eps)
            dgain += jnp.sum(dh_ref[rows, :] * (x * rho), axis=0, keepdims=True)
        turned = jnp.broadcast_to(dgain, (128, x_ref.shape[1])).T
        lane = lax.broadcasted_iota(jnp.int32, turned.shape, 1)
        vectors = jnp.where(lane == 0, turned, vector_ref[...])
        dw_ref[:, dw_ref.shape[1] - 128 :] = vectors.astype(bf16)

def attention_backward(h, x, vectors, q, k, v, do, lse, weight, cos, sin):
    length, width = h.shape
    half = weight.shape[1] // 3
    pairs = half // 128
    full = lambda shape: pl.BlockSpec(shape, lambda p: (0,) * len(shape))
    col = lambda base: pl.BlockSpec((width, 128), lambda p, base=base: (0, base + p))
    out_col = pl.BlockSpec((length, 128), lambda p: (0, p))
    return pl.pallas_call(
        attention_backward_kernel,
        grid=(pairs,),
        in_specs=[full((length, width)), full((length, width)), full((width, 128)), out_col, out_col, out_col, out_col, pl.BlockSpec((1, 2, length), lambda p: (p, 0, 0)), col(0), col(pairs), col(2 * pairs), full((length, 128)), full((length, 128))],
        out_specs=[full((width, 3 * half + 128)), full((length, width))],
        out_shape=[jax.ShapeDtypeStruct((width, 3 * half + 128), bf16), jax.ShapeDtypeStruct((length, width), f32)],
        scratch_shapes=[pltpu.VMEM((length, 128), f32)] * 3,
        compiler_params=pltpu.CompilerParams(vmem_limit_bytes=48 * 2**20),
        cost_estimate=pl.CostEstimate(flops=12 * length * width * half + 10 * length * length * half, bytes_accessed=12 * length * width, transcendentals=length * length * half // HDIM),
    )(h, x, vectors, q, k, v, do, lse, weight, weight, weight, cos, sin)


def gate_columns(value, which):
    high = lax.reduce_precision(value, 8, 7)
    middle = lax.reduce_precision(value - high, 8, 7)
    low = lax.reduce_precision(value - high - middle, 8, 7)
    lane = lax.broadcasted_iota(jnp.int32, (value.shape[0], 128), 1)
    columns = jnp.where(lane == 3, 1.0 * which, 0.0)
    for part, place in ((high, 0), (middle, 1), (low, 2)):
        columns = jnp.where(lane == place + 4 * which, part, columns)
    return columns.astype(bf16)


def expert_kernel(
    flipped_ref,
    taken_ref,
    dout_ref,
    same_ref,
    other_ref,
    f_ref,
    dtaken_ref,
    gradient_ref,
    weight_ref,
    f_acc,
    d_acc,
    dresult_ref,
    taken_turned,
    dresult_turned,
):
    step, last = pl.program_id(0), pl.num_programs(0) - 1
    width = dout_ref.shape[1]

    @pl.when(step == 0)
    def _():
        lanes = taken_ref[:, width:].astype(f32)
        lane = lax.broadcasted_iota(jnp.int32, lanes.shape, 1)
        gate = jnp.sum(jnp.where(lane == 3, 0.0, lanes), axis=1, keepdims=True)
        dresult_ref[...] = (gate * dout_ref[...].astype(f32)).astype(bf16)
        taken_turned[...] = taken_ref[:, :width].T
        dresult_turned[...] = dresult_ref[...].T

    eighth = width // 8
    shift = flipped_ref[0] * eighth
    for matrix in range(3):
        for pair in range(4):
            rows = slice(pair * eighth, (pair + 1) * eighth)
            base = 2 * pair * eighth
            place = pl.ds(pl.multiple_of(base + shift, 32), eighth)
            weight_ref[matrix, place, :] = same_ref[matrix, rows, :]
            place = pl.ds(pl.multiple_of(base + eighth - shift, 32), eighth)
            weight_ref[matrix, place, :] = other_ref[matrix, rows, :]
    taken = taken_ref[:, :width]
    a = dot_nn(taken, weight_ref[0])
    b = dot_nn(taken, weight_ref[1])
    sig = jax.nn.sigmoid(a)
    act = a * sig
    hidden = (act * b).astype(bf16)
    gradient_ref[2] = dot_nn(dresult_turned[...], hidden).astype(bf16)
    dhidden = dot_nn(dresult_ref[...], weight_ref[2])
    dgate = (dhidden * b * (sig * (1.0 + a - act))).astype(bf16)
    dup = (dhidden * act).astype(bf16)
    gradient_ref[0] = dot_nn(taken_turned[...], dgate).astype(bf16)
    gradient_ref[1] = dot_nn(taken_turned[...], dup).astype(bf16)
    f = dot_nt(hidden, weight_ref[2])
    d = dot_nt(dgate, weight_ref[0]) + dot_nt(dup, weight_ref[1])

    @pl.when(step == 0)
    def _():
        f_acc[...] = f
        d_acc[...] = d

    @pl.when(step > 0)
    def _():
        f_acc[...] += f
        d_acc[...] += d

    @pl.when(step == last)
    def _():
        f = f_acc[...].astype(bf16)
        f_ref[...] = f
        dtaken_ref[:, :width] = d_acc[...].astype(bf16)
        dpicked = jnp.sum(dout_ref[...].astype(f32) * f.astype(f32), axis=1, keepdims=True)
        high = dpicked.astype(bf16).astype(f32)
        middle = (dpicked - high).astype(bf16).astype(f32)
        low = (dpicked - high - middle).astype(bf16).astype(f32)
        lanes = taken_ref[:, width:].astype(f32)
        lane = lax.broadcasted_iota(jnp.int32, lanes.shape, 1)
        second = jnp.sum(jnp.where(lane == 3, lanes, 0.0), axis=1, keepdims=True)
        mine = jnp.where(lane < 3, 1.0 - second, jnp.where((lane > 3) & (lane < 7), second, 0.0))
        part = jnp.where(lane % 4 == 0, high, jnp.where(lane % 4 == 1, middle, low))
        dtaken_ref[:, width:] = (mine * part).astype(bf16)


def expert_compute(flipped, taken, dout, same, other):
    rows, width = dout.shape
    hidden = same.shape[2]
    half = pl.BlockSpec((3, width // 2, FF_COLUMNS), lambda i: (0, 0, i))
    whole = lambda columns: pl.BlockSpec((rows, columns), lambda i: (0, 0))
    shape = lambda columns: jax.ShapeDtypeStruct((rows, columns), bf16)
    return pl.pallas_call(
        expert_kernel,
        grid=(hidden // FF_COLUMNS,),
        in_specs=[
            pl.BlockSpec(memory_space=pltpu.SMEM),
            whole(width + 128),
            whole(width),
            half,
            half,
        ],
        out_specs=[
            whole(width),
            whole(width + 128),
            pl.BlockSpec((3, width, FF_COLUMNS), lambda i: (0, 0, i)),
        ],
        out_shape=[
            shape(width),
            shape(width + 128),
            jax.ShapeDtypeStruct((3, width, hidden), bf16),
        ],
        scratch_shapes=[pltpu.VMEM((3, width, FF_COLUMNS), bf16)]
        + [pltpu.VMEM((rows, width), f32)] * 2
        + [pltpu.VMEM((rows, width), bf16)]
        + [pltpu.VMEM((width, rows), bf16)] * 2,
        compiler_params=pltpu.CompilerParams(vmem_limit_bytes=58 * 2**20),
        cost_estimate=pl.CostEstimate(
            flops=20 * rows * width * hidden,
            bytes_accessed=6 * width * hidden + 6 * rows * hidden,
            transcendentals=rows * hidden,
        ),
    )(flipped, taken, dout, same, other)


def make_shards(sizes):
    n_seq, n_x = sizes["seq"], sizes["x"]
    n_dp = sizes["dp_far"] * sizes["dp_near"]

    def shards(
        tokens,
        cotangent,
        previous_logits,
        routes,
        priority,
        attention_master,
        vector_master,
        expert_master,
        mixing_master,
        attention_first,
        vector_first,
        expert_first,
        mixing_first,
        attention_second,
        vector_second,
        expert_second,
        mixing_second,
    ):
        z, y, s = lax.axis_index(DP), lax.axis_index("seq"), lax.axis_index(SHARD)
        far, near = lax.axis_index("dp_far"), lax.axis_index("dp_near")
        x_place, core = lax.axis_index("x"), lax.axis_index("core")
        row_count, model_width = tokens.shape[1], tokens.shape[2]
        half_width = model_width // 2
        local_experts = expert_master.shape[0]
        spread = local_experts == 2 and n_x == 2 and sizes["dp_far"] == 2
        ep_axes = ("dp_near", "seq", "x") if spread else SHARD
        ep_place = lax.axis_index(ep_axes)
        own_rows = attention_master.shape[1]

        def cross(same_y, other_y):
            got = lax.ppermute(same_y, ("dp_near", "core"), [(1, 2), (2, 1)])
            moves = [
                (4 * n + 2 * q + c, 4 * c + 2 * (1 - q) + n)
                for n in range(2)
                for q in range(2)
                for c in range(2)
            ]
            return (
                jnp.where(near == core, same_y, got),
                lax.ppermute(other_y, ("dp_near", "seq", "core"), moves),
            )

        attention_low = attention_master.astype(bf16)
        vector_low = vector_master.astype(bf16).T
        vector_pad = 128 - vector_low.shape[1]

        def weight_pack(which):
            columns = lax.dynamic_slice_in_dim(attention_low[:3], which * half_width, half_width, 2)
            return jnp.concatenate(
                [columns[0], columns[1], columns[2], attention_low[3], jnp.pad(vector_low, ((0, 0), (0, vector_pad)))],
                axis=1,
            )

        packed = in_order(weight_pack(y)[None], swap_seq(weight_pack(1 - y))[None], y, 0)

        packed_z = gather_steps(packed, DP, z, n_dp)
        packed_x = gather_steps(packed_z, "x", x_place, n_x)
        expert_low = after(expert_master, packed).astype(bf16)
        if spread:
            same_y, other_y = cross(*keep_and_send(expert_low, y, 0))
            expert_same = lax.all_gather(
                after(same_y, packed_z), ("dp_far", "core"), axis=1, tiled=True
            )
            expert_other = lax.all_gather(
                after(other_y, packed_z), ("dp_far", "core"), axis=1, tiled=True
            )
            flipped = y
        else:
            expert_use = lax.all_gather(expert_low[0], DP + ("seq",), axis=1, tiled=True)
            expert_use = expert_use.reshape(3, 4, 2, model_width // 8, -1)
            expert_same = expert_use[:, :, 0].reshape(3, model_width // 2, -1)
            expert_other = expert_use[:, :, 1].reshape(3, model_width // 2, -1)
            flipped = jnp.zeros_like(y)

        packed = packed_x
        packed = in_order(packed[None], swap(packed, "core")[None], core, 0)
        packed = packed.transpose(2, 3, 1, 0, 4, 5).reshape(model_width, -1)
        qkv_weight = packed[:, : 3 * half_width]
        out_weight = packed[:, 3 * half_width : 3 * half_width + model_width]
        vector_all = packed[:, 3 * half_width + model_width :][:, : 4 + NEXP].T

        route_rows = routes[0]
        order = priority[0, 0]
        capacity = 9 * row_count * TOP // (8 * NEXP)
        expert_ids = jnp.arange(NEXP)[None, :]
        hit_each = [route_rows[:, j : j + 1] == expert_ids for j in range(TOP)]
        hits = (hit_each[0] | hit_each[1]).astype(bf16)
        before = (order[None, :] < order[:, None]).astype(bf16)
        counts = dot_nn(before, hits)
        kept, dispatch = [], []
        block_ids = jnp.arange(NFFN * capacity)[None, :]
        for j in range(TOP):
            slot = jnp.sum(jnp.where(hit_each[j], counts, 0.0), axis=1, keepdims=True).astype(
                jnp.int32
            )
            route = route_rows[:, j : j + 1]
            keep = (route < NFFN) & (slot < capacity)
            block = ((route // 2) % 2) * 4 + (route % 2) * 2 + route // 4 if spread else route
            block = block ^ ep_place
            kept.append(keep)
            dispatch.append(
                ((block_ids == block * capacity + slot) & keep).astype(bf16)
            )
        dispatch_both = dispatch[0] + dispatch[1]

        tokens_all = in_order(tokens[0], swap_seq(tokens[0]), y, 0)
        gain_one = vector_all[0].astype(f32)[None, :]
        gain_two = vector_all[1].astype(f32)[None, :]
        cosine, sine = rotary_tables(tokens_all.shape[0])
        normed, query, key, value, mixed, log_sums = attention_forward(
            tokens_all, gain_one, qkv_weight, cosine, sine
        )

        upstream = cotangent[0].astype(f32)
        def exchange(rows):
            blocks = rows.reshape(NFFN, capacity, rows.shape[1])
            return [blocks[0]] + [
                lax.ppermute(blocks[k], ep_axes, [(i, i ^ k) for i in range(NFFN)])
                for k in range(1, NFFN)
            ]

        def exchanged(rows):
            return jnp.concatenate(exchange(rows), axis=0)

        dout_rows = dot_tn(dispatch_both, cotangent[0]).astype(bf16)
        dout_rows = exchange(after(dout_rows, tokens_all))
        mixed, dout_rows = lax.optimization_barrier((mixed, dout_rows))

        mixed_keep = lax.dynamic_slice_in_dim(mixed, y * row_count, row_count, 0)
        mixed_send = lax.dynamic_slice_in_dim(mixed, (1 - y) * row_count, row_count, 0)
        mixed_tokens = in_order(mixed_keep, swap_seq(mixed_send), y, 1)

        inputs = tokens[0].astype(f32)
        resid = inputs + dot_nn(mixed_tokens, out_weight)
        rho_two = lax.rsqrt(jnp.mean(resid * resid, axis=-1, keepdims=True) + norm_eps)
        normed_two = resid * rho_two * gain_two
        expert_in = normed_two.astype(bf16)
        router = vector_all[4:]
        previous = previous_logits[0]
        logits = dot_nt(expert_in, router) + exact_dot(previous, mixing_master)
        gates = softmax_rows(logits)
        picked = [
            jnp.sum(jnp.where(hit_each[j], gates, 0.0), axis=1, keepdims=True) for j in range(TOP)
        ]

        consts = vector_all[2:4].astype(f32)
        dlocal = [
            jnp.sum(upstream * normed_two, axis=-1, keepdims=True),
            jnp.sum(upstream * consts[0:1], axis=-1, keepdims=True),
            jnp.sum(upstream * consts[1:2], axis=-1, keepdims=True),
        ]

        taken = dot_tn(
            jnp.concatenate(dispatch, axis=0),
            jnp.concatenate(
                [
                    jnp.concatenate([expert_in, gate_columns(picked[j], j)], axis=1)
                    for j in range(TOP)
                ],
                axis=0,
            ),
        ).astype(bf16)
        taken = exchanged(taken)
        dout_rows = jnp.concatenate(dout_rows, axis=0)
        result, dtaken, dexpert = expert_compute(
            flipped[None].astype(jnp.int32), taken, dout_rows, expert_same, expert_other
        )
        dtaken = exchange(dtaken)
        dtaken = jnp.concatenate(dtaken, axis=0)

        def sum_rows(grad):
            axes = ("dp_far", "core") if spread else DP + ("seq",)
            return lax.psum_scatter(grad, axes, scatter_dimension=1, tiled=True)

        def to_owners(same_y, other_y):
            if not spread:
                return same_y[None]
            same_y, other_y = cross(same_y, other_y)
            return in_order(same_y[None], other_y[None], y, 0)

        result = exchange(after(result, dtaken))
        dexpert = sum_rows(dexpert)
        if spread:
            row_parts = keep_and_send(dexpert.reshape(3, 2, -1, dexpert.shape[2]), y, 1)
        else:
            row_parts = (dexpert, dexpert)


        dgates = jnp.zeros_like(gates)
        returned = dot_nn(dispatch_both, dtaken)
        dnormed_two = returned[:, :model_width]
        value_weight = [0.0, 0.0, 0.0]
        for j in range(TOP):
            route = route_rows[:, j : j + 1]
            local = [jnp.where(route == NFFN + 1 + i, 1.0, 0.0) for i in range(3)]
            parts = returned[:, model_width + 4 * j : model_width + 4 * j + 3]
            dpicked = jnp.sum(parts, axis=1, keepdims=True)
            for i in range(3):
                dpicked = dpicked + jnp.where(route == NFFN + 1 + i, dlocal[i], 0.0)
                value_weight[i] = value_weight[i] + local[i] * picked[j]
            dgates = dgates + jnp.where(hit_each[j], dpicked, 0.0)
        dnormed_two = dnormed_two + value_weight[0] * upstream
        dconst_one = jnp.sum(value_weight[1] * upstream, axis=0, keepdims=True)
        dconst_two = jnp.sum(value_weight[2] * upstream, axis=0, keepdims=True)
        dlogits = gates * (dgates - jnp.sum(gates * dgates, axis=-1, keepdims=True))
        dnormed_two = dnormed_two + exact_dot(dlogits, router.astype(f32))
        drouter = exact_dot(dlogits.T, expert_in.astype(f32))
        dmixing = exact_dot(previous.T, dlogits)
        scaled_two = dnormed_two * gain_two
        dresid = upstream + (
            rho_two * scaled_two
            - resid * (rho_two * rho_two * rho_two) * jnp.mean(resid * scaled_two, -1, keepdims=True)
        )
        dgain_two = jnp.sum(dnormed_two * resid * rho_two, axis=0, keepdims=True)
        dbranch_low = dresid.astype(bf16)
        dweight_out = dot_tn(mixed_tokens, dbranch_low)

        group, place = n_seq * n_x, y * n_x + x_place

        def core_sum(grad):
            grad = grad.astype(bf16).reshape(n_dp, n_seq, n_x, 2, own_rows, -1)
            keep, send = keep_and_send(grad.transpose(3, 1, 2, 0, 4, 5), core, 0)
            return (keep.astype(f32) + swap(send, "core").astype(f32)).astype(bf16)

        def plane_sum(grad):
            grad = grad.reshape((group,) + grad.shape[2:])
            totals = [lax.dynamic_index_in_dim(grad, place, 0, keepdims=False).astype(f32), 0.0]
            for step in range(1, group):
                block = lax.dynamic_index_in_dim(grad, place ^ step, 0, keepdims=False)
                got = lax.ppermute(block, ("seq", "x"), [(i, i ^ step) for i in range(group)])
                totals[step // n_x] = totals[step // n_x] + got.astype(f32)
            return totals

        def dp_sum(grad, wait_for):
            return scatter_steps(after(grad.astype(bf16), wait_for), DP, z, n_dp)

        dmixed = dot_nt(dbranch_low, out_weight).astype(bf16)
        dmixed_keep = lax.dynamic_slice_in_dim(dmixed, y * half_width, half_width, 1)
        dmixed_send = lax.dynamic_slice_in_dim(dmixed, (1 - y) * half_width, half_width, 1)
        dmixed_heads = in_order(dmixed_keep, swap_seq(dmixed_send), y, 0)
        dout_part = core_sum(dweight_out)
        vectors = jnp.concatenate(
            [jnp.zeros_like(dgain_two), dgain_two, dconst_one, dconst_two, drouter], axis=0
        )
        vectors = jnp.pad(vectors.T, ((0, 0), (0, vector_pad)))
        dpack, dnormed_all = attention_backward(
            normed, tokens_all, vectors, query, key, value, dmixed_heads, log_sums, qkv_weight, cosine, sine
        )
        dpack, result = after((dpack, result), dnormed_all)
        dpack = after(dpack, result)
        this_y, other_y = plane_sum(jnp.concatenate([core_sum(dpack), dout_part], axis=-1))
        columns = 3 * half_width
        dpack = dp_sum(
            (
                jnp.concatenate(
                    [
                        this_y[..., :columns],
                        other_y[..., :columns],
                        this_y[..., columns:] + other_y[..., columns:],
                    ],
                    axis=-1,
                ).astype(bf16)
            ),
            row_parts,
        )
        dnormed_keep = lax.dynamic_slice_in_dim(dnormed_all, y * row_count, row_count, 0)
        dnormed_send = lax.dynamic_slice_in_dim(
            after(dnormed_all, this_y), (1 - y) * row_count, row_count, 0
        )
        dnormed = dnormed_keep + swap_seq(dnormed_send.astype(bf16)).astype(f32)
        rho_one = lax.rsqrt(jnp.mean(inputs * inputs, axis=-1, keepdims=True) + norm_eps)
        scaled_one = dnormed * gain_one
        input_gradient = dresid + (
            rho_one * scaled_one
            - inputs * (rho_one * rho_one * rho_one) * jnp.mean(inputs * scaled_one, -1, keepdims=True)
        )
        dpack = after(dpack, dexpert)
        result = jnp.concatenate(result, axis=0)
        mixture = (
            picked[0] * dot_nn(dispatch[0], result)
            + picked[1] * dot_nn(dispatch[1], result)
            + value_weight[0] * normed_two
            + value_weight[1] * consts[0:1]
            + value_weight[2] * consts[1:2]
        )
        block_output = (resid + mixture).astype(bf16)
        dpack = with_layout_constraint(dpack, Layout((0, 1)))
        head_pairs = half_width // 128

        def by_matrix(part):
            return jnp.stack(
                [
                    jnp.concatenate(
                        [
                            part[:, 384 * pair + 128 * which : 384 * pair + 128 * which + 128]
                            for pair in range(head_pairs)
                        ],
                        axis=1,
                    )
                    for which in range(3)
                ]
            )

        qkv_sum = in_order(
            by_matrix(dpack[:, :columns]), by_matrix(dpack[:, columns : 2 * columns]), y, 2
        )
        vector_sum = dpack[:, 2 * columns :][:, : 4 + NEXP].T
        dout_sum = dpack[:, 2 * columns + 128 :]
        attention_sum = jnp.concatenate([qkv_sum, dout_sum[None]], axis=0)

        attention_m, attention_s, attention_u = moments(
            attention_master, attention_first, attention_second, attention_sum
        )
        vector_m, vector_s, vector_u = moments(
            vector_master, vector_first, vector_second, vector_sum
        )
        expert_sum = to_owners(*row_parts).astype(f32)
        expert_m, expert_s, expert_u = moments(
            expert_master, expert_first, expert_second, expert_sum
        )

        expert_kept = lax.optimization_barrier(expert_u.astype(bf16)).astype(f32)

        def squares(attention_x, vector_x, expert_x):
            vector_parts = jnp.sum(vector_x * vector_x, axis=1)
            expert_parts = lax.dynamic_update_slice_in_dim(
                jnp.zeros((NFFN * 3,), f32),
                jnp.sum(expert_x * expert_x, axis=(2, 3)).reshape(-1),
                s * local_experts * 3,
                0,
            )
            return jnp.concatenate(
                [
                    jnp.sum(attention_x * attention_x, axis=(1, 2)),
                    vector_parts[0:2],
                    jnp.sum(vector_parts[2:4])[None],
                    jnp.sum(vector_parts[4:])[None],
                    expert_parts,
                ]
            )

        count = 8 + 3 * NFFN
        small = jnp.concatenate(
            [
                squares(attention_master, vector_master, expert_master),
                squares(attention_u, vector_u, expert_u),
                dmixing.reshape(-1),
            ]
        )
        used = small.shape[0]
        small = jnp.pad(small, (0, -used % 128)).reshape(-1, 128)
        small = sum_everywhere(small, sizes).reshape(-1)
        summed_squares = small[: 2 * count].reshape(2, count)
        mixing_grad = small[2 * count : used].reshape(NEXP, NEXP)
        mixing_m, mixing_s, mixing_u = moments(
            mixing_master, mixing_first, mixing_second, mixing_grad
        )
        mixing_squares = jnp.stack(
            [jnp.sum(mixing_master * mixing_master), jnp.sum(mixing_u * mixing_u)]
        )
        tensor_norms = jnp.sqrt(jnp.concatenate([summed_squares, mixing_squares[:, None]], axis=1))
        ratios = learn_rate * (tensor_norms[0] / (tensor_norms[1] + norm_eps))
        vector_ratio = jnp.concatenate(
            [
                ratios[4:6],
                jnp.broadcast_to(ratios[6:7], (2,)),
                jnp.broadcast_to(ratios[7:8], (NEXP,)),
            ]
        )[:, None]
        expert_ratio = lax.dynamic_slice_in_dim(
            ratios[8:count].reshape(NFFN, 3), s * local_experts, local_experts, 0
        )[:, :, None, None]
        return (
            block_output[None],
            input_gradient[None],
            attention_master - ratios[0:4][:, None, None] * attention_u,
            vector_master - vector_ratio * vector_u,
            expert_master - expert_ratio * expert_kept,
            mixing_master - ratios[count] * mixing_u,
            attention_m,
            vector_m,
            expert_m,
            mixing_m,
            attention_s,
            vector_s,
            expert_s,
            mixing_s,
            tensor_norms,
        )

    return shards


def solution(mesh):
    n_dp, n_seq, n_shard = (mesh.shape[name] for name in ("dp", "seq", "shard"))
    finer = jax.sharding.Mesh(
        mesh.devices.reshape(n_dp // 2, 2, n_seq, n_shard // 2, 2), DP + ("seq",) + SHARD
    )
    tokens_spec = P(DP + SHARD, "seq", None)
    attention_spec = P(None, DP + ("seq",) + SHARD, None)
    vector_spec = P(None, DP + ("seq",) + SHARD)
    expert_spec = P(SHARD, None, DP + ("seq",), None)
    weights = (attention_spec, vector_spec, expert_spec, P())
    return jax.shard_map(
        make_shards(dict(finer.shape)),
        mesh=finer,
        in_specs=(tokens_spec,) * 5 + weights * 3,
        out_specs=(tokens_spec,) * 2 + weights * 3 + (P(),),
        check_vma=False,
    )
```
